256 devices in a mesh: geo: 64 (over z, y, core), spec: 4 (over x).
Axes of the slice: x: 4, y: 4, z: 8, core: 2. Of those that a mesh axis runs over, the one named last changes fastest.
Arguments:
- spectrum: float32 [50, 36, 128, 512], P(None, None, 'geo', 'spec'), may hold values from 0.05 to 1
- wind_speed: float32 [128, 512], P('geo', 'spec'), may hold values from 5 to 20
- wind_dir: float32 [128, 512], P('geo', 'spec'), may hold values from -3.140625 to 3.140625
- current_u: float32 [128, 512], P('geo'), may hold values from -1 to 1
- current_v: float32 [128, 512], P('geo'), may hold values from -1 to 1
- refract_x: float32 [128, 512], P('geo'), may hold values from -1e-05 to 1e-05
- refract_y: float32 [128, 512], P('geo'), may hold values from -1e-05 to 1e-05
- land_mask: int32 [128, 512], P('geo'), may hold values 0 or 1
Outputs:
- new_spectrum: float32 [50, 36, 128, 512], P(None, None, 'geo', 'spec')
The draws below stay inside these ranges and needn't reach their ends.
All inputs are finite; a program needn't handle non-finite values. No bound on the sum of `land_mask` on one device may be relied on, other than what follows from the above.
Results may differ from the reference program's by a relative error of at most 0.00015.
Values sent between devices are 32-bit elements; how exact they have to be, the bound alone decides.
No kernel may reach another device: no remote copies, remote signals or barrier semaphores. Data moves between devices by JAX's collectives and lax.ppermute only.
A program may use at most 128 MiB of HBM per device.

```python
import math
import jax
import jax.numpy as jnp
from jax import lax

NFREQ = 50
NDIR = 36
NCOL = 512
NSUB = 2
NROWS = 128


def set_ends(drawn, key, smallest, top_value):
    longest = drawn.shape.index(max(drawn.shape))
    spots = []
    for shift in (0, 1):
        where = [jax.random.randint(jax.random.fold_in(key, axis), (), 0, length) for axis, length in enumerate(drawn.shape)]
        where[longest] = (where[longest] + shift) % drawn.shape[longest]
        spots.append(tuple(where))
    return drawn.at[spots[0]].set(smallest).at[spots[1]].set(top_value)


def steps_of(stream_key, shape, split, smallest, top_value):
    factor_of = 1.0
    for axis_at, parts in split:
        draws = jax.random.uniform(jax.random.fold_in(jax.random.fold_in(stream_key, 6), axis_at), (parts,), jnp.float32, smallest / len(split), top_value / len(split))
        factor_of = factor_of * jnp.repeat(jnp.exp(draws), shape[axis_at] // parts).reshape((-1,) + (1,) * (len(shape) - 1 - axis_at))
    return factor_of


def setup_inputs(seed: int = 0) -> dict:
    splits = jax.random.split(jax.random.key(seed), 9)
    return {
        "spectrum": jnp.clip(jnp.exp(math.log(1.0) - 2.9957323 * jax.random.uniform(splits[0], (NFREQ, NDIR, NROWS, NCOL), jnp.float32) ** steps_of(splits[0], (NFREQ, NDIR, NROWS, NCOL), ((2, 64), (3, 4)), -0.2, 0.2)), 0.05, 1.0),
        "wind_speed": jnp.clip(5.0 + 15.0 * jax.random.uniform(splits[1], (NROWS, NCOL), jnp.float32) ** steps_of(splits[1], (NROWS, NCOL), ((0, 64), (1, 4)), -0.2, 0.2), 5.0, 20.0),
        "wind_dir": jnp.clip(jax.random.uniform(splits[2], (NROWS, NCOL), jnp.float32, -3.140625, 3.140625), -3.140625, 3.140625),
        "current_u": jnp.clip(jax.random.uniform(splits[3], (NROWS, NCOL), jnp.float32, -1.0, 1.0) * steps_of(splits[3], (NROWS, NCOL), ((0, 64),), -0.4, 0.0), -1.0, 1.0),
        "current_v": jnp.clip(jax.random.uniform(splits[4], (NROWS, NCOL), jnp.float32, -1.0, 1.0) * steps_of(splits[4], (NROWS, NCOL), ((0, 64),), -0.4, 0.0), -1.0, 1.0),
        "refract_x": jnp.clip(jax.random.uniform(splits[5], (NROWS, NCOL), jnp.float32, -9.999999747378752e-06, 9.999999747378752e-06) * steps_of(splits[5], (NROWS, NCOL), ((0, 64),), -0.4, 0.0), -9.999999747378752e-06, 9.999999747378752e-06),
        "refract_y": jnp.clip(jax.random.uniform(splits[6], (NROWS, NCOL), jnp.float32, -9.999999747378752e-06, 9.999999747378752e-06) * steps_of(splits[6], (NROWS, NCOL), ((0, 64),), -0.4, 0.0), -9.999999747378752e-06, 9.999999747378752e-06),
        "land_mask": set_ends((jax.random.randint(splits[7], (NROWS, NCOL), 0, 4) < 3).astype(jnp.int32), jax.random.fold_in(splits[7], 1), 0, 1),
    }


gravity = 9.81
lowest_radian = 2.0 * math.pi * 0.0373
log_span = 49.0 * math.log(1.1)
wind_coef = 1.7e-6
break_coef = 2.5e-5
steep_ref = 480.0
wind_factor = 1.1
source_seconds = 360.0
courant_cells = 0.02
substep_seconds = 180.0


def tables(nfreq, ndir):
    ratio = log_span / (nfreq - 1)
    radian_freq = lowest_radian * jnp.exp(jnp.arange(nfreq, dtype=jnp.float32) * ratio)
    band_width = radian_freq * (math.exp(ratio) - 1.0)
    dir_width = 2.0 * math.pi / ndir
    angles = jnp.arange(ndir, dtype=jnp.float32) * dir_width
    return radian_freq, band_width, angles, dir_width


def statistics(energy_total, inverse):
    mean_sigma = energy_total / inverse
    mean_k = mean_sigma * mean_sigma / gravity
    steepness = energy_total * mean_k * mean_k
    return mean_sigma, steepness


def source_plane(freq_plane, radian, cos_dir, sin_dir, wind_speed, wind_dir, mean_sigma, steepness, sea_cells):
    alignment = cos_dir * jnp.cos(wind_dir) + sin_dir * jnp.sin(wind_dir)
    growth = wind_coef * radian * jnp.maximum(wind_factor * wind_speed * radian / gravity * alignment - 1.0, 0.0)
    ratio = steepness / steep_ref
    dissipation = break_coef * ratio * ratio * radian * radian / mean_sigma
    return sea_cells * freq_plane * (1.0 + source_seconds * growth) / (1.0 + source_seconds * dissipation)


def advect(energy, speed, courant, axis_dim, from_below, from_above):
    q_plus = courant * jnp.maximum(speed, 0.0) * energy
    q_minus = courant * jnp.minimum(speed, 0.0) * energy
    length = energy.shape[axis_dim]
    below_rim = from_below(lax.slice_in_dim(q_plus, length - 1, length, axis=axis_dim))
    above_rim = from_above(lax.slice_in_dim(q_minus, 0, 1, axis=axis_dim))
    inflow = jnp.concatenate([below_rim, lax.slice_in_dim(q_plus, 0, length - 1, axis=axis_dim)], axis=axis_dim)
    outflow = jnp.concatenate([lax.slice_in_dim(q_minus, 1, length, axis=axis_dim), above_rim], axis=axis_dim)
    return inflow - outflow - q_plus + q_minus


def transport_step(energy, group_speed, cos_dir, sin_dir, current_u, current_v, refract_x, refract_y, sea_cells, dir_courant, axis_dims, col_pair, row_pair, dir_pair):
    speed_x = group_speed * cos_dir + current_u
    speed_y = group_speed * sin_dir + current_v
    speed_t = group_speed * (sin_dir * refract_x - cos_dir * refract_y)
    change_x = advect(energy, speed_x, courant_cells, axis_dims[2], col_pair[0], col_pair[1])
    change_y = advect(energy, speed_y, courant_cells, axis_dims[1], row_pair[0], row_pair[1])
    change_t = advect(energy, speed_t, dir_courant, axis_dims[0], dir_pair[0], dir_pair[1])
    return sea_cells * (energy + change_x + change_y + change_t)


def nothing_beyond(rim_slice):
    return jnp.zeros_like(rim_slice)


def wrap_around(rim_slice):
    return rim_slice


def reference(spectrum, wind_speed, wind_dir, current_u, current_v, refract_x, refract_y, land_mask):
    radian_freq, band_width, angles, dir_width = tables(NFREQ, NDIR)
    sea_cells = land_mask.astype(jnp.float32)
    cos_dir = jnp.cos(angles)[:, None, None]
    sin_dir = jnp.sin(angles)[:, None, None]
    dir_courant = substep_seconds / dir_width

    def accumulate(running, inputs):
        freq_plane, radian, band = inputs
        weight = band * dir_width
        return (running[0] + jnp.sum(freq_plane * weight, axis=0), running[1] + jnp.sum(freq_plane * (weight / radian), axis=0)), None

    blank_field = jnp.zeros(wind_speed.shape, jnp.float32)
    (energy_total, inverse), _ = lax.scan(accumulate, (blank_field, blank_field), (spectrum, radian_freq, band_width))
    mean_sigma, steepness = statistics(energy_total, inverse)

    def one_freq(inputs):
        freq_plane, radian = inputs
        energy = source_plane(freq_plane, radian, cos_dir, sin_dir, wind_speed, wind_dir, mean_sigma, steepness, sea_cells)
        group_speed = gravity / (2.0 * radian)
        for substep in range(NSUB):
            energy = transport_step(energy, group_speed, cos_dir, sin_dir, current_u, current_v, refract_x, refract_y, sea_cells, dir_courant, (0, 1, 2), (nothing_beyond, nothing_beyond), (nothing_beyond, nothing_beyond), (wrap_around, wrap_around))
        return energy

    return lax.map(one_freq, (spectrum, radian_freq))
```

```python
import functools
import math

import jax
import jax.numpy as jnp
from jax import lax
from jax.experimental import pallas as pl
from jax.experimental.pallas import tpu as pltpu
from jax.sharding import PartitionSpec as P

gravity = 9.81
lowest_radian = 2.0 * math.pi * 0.0373
log_span = 49.0 * math.log(1.1)
wind_coef = 1.7e-06
break_coef = 2.5e-05
steep_ref = 480.0
wind_factor = 1.1
source_seconds = 360.0
courant_cells = 0.02
substep_seconds = 180.0

NF = 50
ND = 36
LANES = 128
SUB = 8
GROUPS = 7
PADF = SUB * GROUPS
RATIO = log_span / (NF - 1)
DTH = 2.0 * math.pi / ND
COS = [math.cos(DTH * i) for i in range(ND)]
SIN = [math.sin(DTH * i) for i in range(ND)]
GSPEED = [gravity / (2.0 * lowest_radian * math.exp(RATIO * j)) for j in range(NF)]
FIRST = [
    min(j for j in range(NF) if GSPEED[j] * SIN[i] > -1.001) // SUB for i in range(ND)
]
RANK = [0] * ND
for place, i_of in enumerate(sorted(range(ND), key=lambda i: (FIRST[i], i))):
    RANK[i_of] = place
COUNT = [sum(1 for i in range(ND) if FIRST[i] <= g) for g in range(GROUPS)]
BASE = [SUB * sum(COUNT[:g]) for g in range(GROUPS)]
SPARE = SUB * sum(COUNT)
PACKET = SPARE + SUB
FIELD = 2 * ND * PADF
SIDE = 2 * PADF
F32 = jnp.float32


def mirrored(i):
    return (ND - i) % ND


def group_base(group):
    total = 0
    for g in range(GROUPS - 1):
        total = total + jnp.where(group > g, SUB * COUNT[g], 0)
    return total


def slot(base, group, i):
    place = base + SUB * RANK[i]
    if FIRST[i] > 0:
        place = jnp.where(group >= FIRST[i], place, SPARE)
    return pl.ds(pl.multiple_of(place, SUB), SUB)


def field_rows(group, r, i):
    return pl.ds(pl.multiple_of((r * ND + i) * PADF + group * SUB, SUB), SUB)


def side_rows(group, r):
    return pl.ds(pl.multiple_of(r * PADF + group * SUB, SUB), SUB)


def radian_of(group):
    j = lax.broadcasted_iota(jnp.int32, (SUB, LANES), 0) + group * SUB
    return lowest_radian * jnp.exp(j.astype(F32) * RATIO), j


def position():
    odd = lax.rem(lax.axis_index("geo"), 2)
    col = pl.multiple_of(lax.axis_index("spec") * LANES, LANES)
    sign = jnp.where(odd == 1, -1.0, 1.0).astype(F32)
    return odd, col, sign


def row_of(ref, odd, r, col):
    window = (ref[...] if col is None else ref[:, pl.ds(col, LANES)]).astype(F32)
    first, second = window[0:1], window[1:2]
    own, other = (first, second) if r == 0 else (second, first)
    return jnp.where(odd == 1, other, own)


def spread(row):
    return jnp.broadcast_to(row, (SUB, LANES))


def lane_ids():
    return lax.broadcasted_iota(jnp.int32, (SUB, LANES), 1)


def emit(group, base, i, energy, cx, cy, lane, pair, gather, cross_ref, chip_ref):
    cross_ref[slot(base, group, mirrored(i)), :] = jnp.maximum(-cy[0], 0.0) * energy[0]
    chip_ref[slot(base, group, i), :] = jnp.maximum(cy[1], 0.0) * energy[1]
    out = []
    for r in range(2):
        speed = jnp.where(lane == 0, jnp.minimum(cx[r], 0.0), jnp.maximum(cx[r], 0.0))
        moved = pltpu.roll(speed * energy[r], 2 * i + 2, 1)
        out.append(jnp.where(pair == i + 1, moved, gather[r]))
    return out


def finish_packets(cross_ref, chip_ref):
    blank = jnp.zeros((SUB, LANES), F32)
    cross_ref[SPARE:PACKET, :] = blank
    chip_ref[SPARE:PACKET, :] = blank


def source_kernel(
    spec_hbm, ws_ref, wd_ref, u_ref, v_ref, sea_ref, e_ref, cross_ref, chip_ref, side_ref, raw, sem
):
    odd, col, sign = position()
    copy = pltpu.make_async_copy(spec_hbm, raw.at[pl.ds(0, NF * 2 * ND)], sem)
    copy.start()
    raw[NF * 2 * ND :, :] = jnp.zeros(((PADF - NF) * 2 * ND, LANES), F32)
    copy.wait()

    def stats(group, sums):
        s, j = radian_of(group)
        valid = j < NF
        w1 = jnp.where(valid, s * ((math.exp(RATIO) - 1.0) * DTH), 0.0)
        w2 = jnp.where(valid, (math.exp(RATIO) - 1.0) * DTH, 0.0)
        out = []
        for r in range(2):
            parts = [None, None, None, None]
            r_from = jnp.where(odd == 1, 1 - r, r)
            for i in range(ND):
                i_from = jnp.where(odd == 1, 2 * mirrored(i), 2 * i)
                got = raw[pl.ds(group * (SUB * 2 * ND) + i_from + r_from, SUB, stride=2 * ND), :]
                e_ref[field_rows(group, r, i), :] = got
                k = i % 4
                parts[k] = got if parts[k] is None else parts[k] + got
            part = (parts[0] + parts[1]) + (parts[2] + parts[3])
            out.append((sums[r][0] + part * w1, sums[r][1] + part * w2))
        return tuple(out)

    blank = jnp.zeros((SUB, LANES), F32)
    sums = lax.fori_loop(0, GROUPS, stats, ((blank, blank), (blank, blank)))
    wind_x, wind_y, sea, decay, u, v = [], [], [], [], [], []
    for r in range(2):
        total = jnp.sum(sums[r][0], axis=0, keepdims=True)
        inverse = jnp.sum(sums[r][1], axis=0, keepdims=True)
        mean_sigma = total / inverse
        mean_k = mean_sigma * mean_sigma / gravity
        ratio = total * mean_k * mean_k / steep_ref
        decay.append(spread(source_seconds * break_coef * ratio * ratio / mean_sigma))
        strength = row_of(ws_ref, odd, r, None) * (wind_factor / gravity)
        angle = row_of(wd_ref, odd, r, None) * sign
        wind_x.append(spread(strength * jnp.cos(angle)))
        wind_y.append(spread(strength * jnp.sin(angle)))
        sea.append(spread(row_of(sea_ref, odd, r, col)))
        u.append(spread(courant_cells * row_of(u_ref, odd, r, col)))
        v.append(spread(courant_cells * sign * row_of(v_ref, odd, r, col)))
    lane = lane_ids()
    pair = lax.shift_right_logical(lane + 1, 1)

    def source(group, carry):
        s, _ = radian_of(group)
        fc = (courant_cells * gravity / 2.0) / s
        gain = s * (source_seconds * wind_coef)
        damp = [sea[r] / (1.0 + decay[r] * s * s) for r in range(2)]
        base = group_base(group)
        gather = [blank, blank]
        for i in range(ND):
            energy, cx, cy = [], [], []
            for r in range(2):
                rows = field_rows(group, r, i)
                align = wind_x[r] * COS[i] + wind_y[r] * SIN[i]
                growth = gain * jnp.maximum(s * align - 1.0, 0.0)
                new = e_ref[rows, :] * damp[r] * (1.0 + growth)
                e_ref[rows, :] = new
                energy.append(new)
                cx.append(fc * COS[i] + u[r])
                cy.append(fc * SIN[i] + v[r])
            gather = emit(
                group, base, i, energy, cx, cy, lane, pair, gather, cross_ref, chip_ref
            )
        for r in range(2):
            side_ref[side_rows(group, r), :] = gather[r]
        return carry

    lax.fori_loop(0, GROUPS, source, 0)
    finish_packets(cross_ref, chip_ref)


def transport_kernel(
    last, e_ref, cross_in, chip_in, west_in, east_in, u_ref, v_ref, rx_ref, ry_ref, sea_ref, *rest
):
    if last:
        out_hbm, work, turn, sem = rest
    else:
        out_ref, cross_ref, chip_ref, side_ref, turn = rest
    odd, col, sign = position()
    sea, u, v = [], [], []
    for r in range(2):
        sea.append(spread(row_of(sea_ref, odd, r, col)))
        u.append(spread(courant_cells * row_of(u_ref, odd, r, col)))
        v.append(spread(courant_cells * sign * row_of(v_ref, odd, r, col)))
        rx = row_of(rx_ref, odd, r, col)
        ry = sign * row_of(ry_ref, odd, r, col)
        for i in range(ND):
            turn[r * ND + i : r * ND + i + 1, :] = SIN[i] * rx - COS[i] * ry
    lane = lane_ids()
    pair = lax.shift_right_logical(lane + 1, 1)
    odd_lane = lax.rem(lane, 2) == 1
    blank = jnp.zeros((SUB, LANES), F32)

    def substep(group, carry):
        s, _ = radian_of(group)
        c = (gravity / 2.0) / s
        fc = courant_cells * c
        tc = (substep_seconds / DTH) * c
        base = group_base(group)
        border = []
        for r in range(2):
            rows = side_rows(group, r)
            border.append(
                jnp.where(odd_lane, west_in[rows, :], pltpu.roll(east_in[rows, :], LANES - 2, 1))
            )

        def turned(r, i):
            energy = e_ref[field_rows(group, r, i), :]
            speed = tc * spread(turn[r * ND + i : r * ND + i + 1, :])
            return energy, jnp.maximum(speed, 0.0) * energy, jnp.minimum(speed, 0.0) * energy

        before = [turned(r, ND - 1)[1] for r in range(2)]
        first = [turned(r, 0) for r in range(2)]
        here = first
        gather = [blank, blank]
        for i in range(ND):
            after = [turned(r, i + 1) for r in range(2)] if i + 1 < ND else first
            cx = [fc * COS[i] + u[r] for r in range(2)]
            cy = [fc * SIN[i] + v[r] for r in range(2)]
            energy = [here[r][0] for r in range(2)]
            py = [jnp.maximum(cy[r], 0.0) * energy[r] for r in range(2)]
            my = [jnp.minimum(cy[r], 0.0) * energy[r] for r in range(2)]
            from_cross = cross_in[slot(base, group, i), :]
            from_chip = chip_in[slot(base, group, mirrored(i)), :]
            in_y = [from_cross - my[1], py[0] + from_chip]
            new = []
            for r in range(2):
                px = jnp.maximum(cx[r], 0.0) * energy[r]
                mx = jnp.minimum(cx[r], 0.0) * energy[r]
                brought = pltpu.roll(border[r], (LANES - (2 * i + 1)) % LANES, 1)
                px_in = jnp.where(lane == 0, brought, pltpu.roll(px, 1, 1))
                mx_in = jnp.where(lane == LANES - 1, brought, pltpu.roll(mx, LANES - 1, 1))
                stay = energy[r] - (px - mx) - (py[r] - my[r]) - (here[r][1] - here[r][2])
                gained = (px_in - mx_in) + in_y[r] + (before[r] - after[r][2])
                new.append(sea[r] * (stay + gained))
            if last:
                for r in range(2):
                    i_to = jnp.where(odd == 1, 2 * mirrored(i), 2 * i)
                    r_to = jnp.where(odd == 1, 1 - r, r)
                    work[pl.ds(group * (SUB * 2 * ND) + i_to + r_to, SUB, stride=2 * ND), :] = new[r]
            else:
                for r in range(2):
                    out_ref[field_rows(group, r, i), :] = new[r]
                gather = emit(
                    group, base, i, new, cx, cy, lane, pair, gather, cross_ref, chip_ref
                )
            before = [here[r][1] for r in range(2)]
            here = after
        if not last:
            for r in range(2):
                side_ref[side_rows(group, r), :] = gather[r]
        return carry

    lax.fori_loop(0, GROUPS, substep, 0)
    if last:
        copy = pltpu.make_async_copy(work.at[pl.ds(0, NF * 2 * ND)], out_hbm, sem)
        copy.start()
        copy.wait()
    else:
        finish_packets(cross_ref, chip_ref)


VMEM = pl.BlockSpec(memory_space=pltpu.VMEM)
ANY = pl.BlockSpec(memory_space=pl.ANY)
PARAMS = pltpu.CompilerParams(vmem_limit_bytes=24 * 1024 * 1024)


def packets():
    return [
        jax.ShapeDtypeStruct((FIELD, LANES), F32),
        jax.ShapeDtypeStruct((PACKET, LANES), F32),
        jax.ShapeDtypeStruct((PACKET, LANES), F32),
        jax.ShapeDtypeStruct((SIDE, LANES), F32),
    ]


def exchange(cross, chip, side):
    geo, spec = lax.axis_size("geo"), lax.axis_size("spec")
    links = [(k, k + 1) for k in range(1, geo - 1, 2)]
    cores = [(k, k + 1) for k in range(0, geo, 2)]
    east = [(k, k + 1) for k in range(spec - 1)]
    both = lambda pairs: pairs + [(b, a) for a, b in pairs]
    return (
        lax.ppermute(cross, "geo", both(links)),
        lax.ppermute(chip, "geo", both(cores)),
        lax.ppermute(side, "spec", east),
        lax.ppermute(side, "spec", [(b, a) for a, b in east]),
    )


def per_device(
    spectrum, wind_speed, wind_dir, current_u, current_v, refract_x, refract_y, land_mask
):
    rows = spectrum.shape[0] * spectrum.shape[1] * spectrum.shape[2]
    flat = spectrum.reshape(rows, LANES)
    energy, cross, chip, side = pl.pallas_call(
        source_kernel,
        out_shape=packets(),
        in_specs=[ANY] + [VMEM] * 5,
        out_specs=[VMEM] * 4,
        scratch_shapes=[pltpu.VMEM((PADF * 2 * ND, LANES), F32), pltpu.SemaphoreType.DMA],
        compiler_params=PARAMS,
        name="source",
    )(flat, wind_speed, wind_dir, current_u, current_v, land_mask)
    halo = exchange(cross, chip, side)
    energy, cross, chip, side = pl.pallas_call(
        functools.partial(transport_kernel, False),
        out_shape=packets(),
        in_specs=[VMEM] * 10,
        out_specs=[VMEM] * 4,
        scratch_shapes=[pltpu.VMEM((2 * ND, LANES), F32)],
        compiler_params=PARAMS,
        name="first_substep",
    )(energy, *halo, current_u, current_v, refract_x, refract_y, land_mask)
    halo = exchange(cross, chip, side)
    out = pl.pallas_call(
        functools.partial(transport_kernel, True),
        out_shape=jax.ShapeDtypeStruct((rows, LANES), F32),
        in_specs=[VMEM] * 10,
        out_specs=ANY,
        scratch_shapes=[
            pltpu.VMEM((PADF * 2 * ND, LANES), F32),
            pltpu.VMEM((2 * ND, LANES), F32),
            pltpu.SemaphoreType.DMA,
        ],
        compiler_params=PARAMS,
        name="second_substep",
    )(energy, *halo, current_u, current_v, refract_x, refract_y, land_mask)
    return out.reshape(spectrum.shape)


def solution(mesh):
    in_specs = (
        P(None, None, "geo", "spec"),
        P("geo", "spec"),
        P("geo", "spec"),
        P("geo", None),
        P("geo", None),
        P("geo", None),
        P("geo", None),
        P("geo", None),
    )
    out_specs = P(None, None, "geo", "spec")
    return jax.shard_map(
        per_device, mesh=mesh, in_specs=in_specs, out_specs=out_specs, check_vma=False
    )
```

```python
import functools
import math

import jax
import jax.numpy as jnp
from jax import lax
from jax.experimental import pallas as pl
from jax.experimental.pallas import tpu as pltpu
from jax.sharding import PartitionSpec as P

gravity = 9.81
lowest_radian = 2.0 * math.pi * 0.0373
log_span = 49.0 * math.log(1.1)
wind_coef = 1.7e-06
break_coef = 2.5e-05
steep_ref = 480.0
wind_factor = 1.1
source_seconds = 360.0
courant_cells = 0.02
substep_seconds = 180.0

NF = 50
ND = 36
LANES = 128
SUB = 8
GROUPS = 7
PADF = SUB * GROUPS
RATIO = log_span / (NF - 1)
DTH = 2.0 * math.pi / ND
COS = [math.cos(DTH * i) for i in range(ND)]
SIN = [math.sin(DTH * i) for i in range(ND)]
GSPEED = [gravity / (2.0 * lowest_radian * math.exp(RATIO * j)) for j in range(NF)]
FIRST = [
    min(j for j in range(NF) if GSPEED[j] * SIN[i] > -1.001) // SUB for i in range(ND)
]
RANK = [0] * ND
for place, i_of in enumerate(sorted(range(ND), key=lambda i: (FIRST[i], i))):
    RANK[i_of] = place
COUNT = [sum(1 for i in range(ND) if FIRST[i] <= g) for g in range(GROUPS)]
BASE = [SUB * sum(COUNT[:g]) for g in range(GROUPS)]
TAIL = NF - SUB * (GROUPS - 1)
FIT = SUB // TAIL
SPARE = BASE[-1] + SUB * (ND // FIT)
PACKET = SPARE + SUB
TURN = 8
FIELDS = TURN + 2 * ND
BATCH = 3
CHUNK = SUB * 2 * ND
FIELD = 2 * ND * PADF
SIDE = 2 * PADF
F32 = jnp.float32


def mirrored(i):
    return (ND - i) % ND


LAST = GROUPS - 1


def group_base(group):
    if group is LAST:
        return BASE[-1]
    total = 0
    for g in range(GROUPS - 1):
        total = total + jnp.where(group > g, SUB * COUNT[g], 0)
    return total


def slot(base, group, i):
    place = base + SUB * RANK[i]
    if FIRST[i] > 0:
        place = jnp.where(group >= FIRST[i], place, SPARE)
    return aligned(place)


def aligned(start):
    return pl.ds(start if isinstance(start, int) else pl.multiple_of(start, SUB), SUB)


def field_rows(group, r, i):
    return aligned((r * ND + i) * PADF + group * SUB)


def side_rows(group, r):
    return aligned(r * PADF + group * SUB)


def fetch(ref, group, base, i):
    if group is LAST:
        got = ref[aligned(BASE[-1] + SUB * (RANK[i] // FIT)), :]
        return pltpu.roll(got, (SUB - TAIL * (RANK[i] % FIT)) % SUB, 0)
    return ref[slot(base, group, i), :]


class Sender:
    def __init__(self, ref, group, base):
        self.ref, self.group, self.base, self.shared = ref, group, base, {}

    def put(self, i, value):
        if self.group is not LAST:
            return [(self.ref, slot(self.base, self.group, i), value)]
        block, part = RANK[i] // FIT, RANK[i] % FIT
        held = self.shared.setdefault(block, {})
        held[part] = pltpu.roll(value, TAIL * part, 0) if part else value
        if len(held) < FIT:
            return []
        place = lax.broadcasted_iota(jnp.int32, (SUB, LANES), 0)
        full = held[FIT - 1]
        for part in range(FIT - 1):
            inside = (place >= TAIL * part) & (place < TAIL * (part + 1))
            full = jnp.where(inside, held[part], full)
        return [(self.ref, aligned(BASE[-1] + SUB * block), full)]


def radian_of(group):
    j = lax.broadcasted_iota(jnp.int32, (SUB, LANES), 0) + group * SUB
    return lowest_radian * jnp.exp(j.astype(F32) * RATIO), j


def position():
    odd = lax.rem(lax.axis_index("geo"), 2)
    col = pl.multiple_of(lax.axis_index("spec") * LANES, LANES)
    sign = jnp.where(odd == 1, -1.0, 1.0).astype(F32)
    return odd, col, sign


def row_of(ref, odd, r, col):
    window = (ref[...] if col is None else ref[:, pl.ds(col, LANES)]).astype(F32)
    first, second = window[0:1], window[1:2]
    own, other = (first, second) if r == 0 else (second, first)
    return jnp.where(odd == 1, other, own)


def spread(row):
    return jnp.broadcast_to(row, (SUB, LANES))


def lane_ids():
    return lax.broadcasted_iota(jnp.int32, (SUB, LANES), 1)


class Gather:
    def __init__(self, lane):
        self.lane, self.pair = lane, lax.shift_right_logical(lane + 1, 1)
        self.total = [jnp.zeros((SUB, LANES), F32)] * 2
        self.queue = []

    def put(self, i, energy, cx):
        flux = []
        for r in range(2):
            speed = jnp.where(self.lane == 0, jnp.minimum(cx[r], 0.0), jnp.maximum(cx[r], 0.0))
            flux.append(speed * energy[r])
        self.queue.append((i, flux))

    def finish(self, side_ref, group):
        for i, flux in self.queue:
            for r in range(2):
                moved = pltpu.roll(flux[r], 2 * i + 2, 1)
                self.total[r] = jnp.where(self.pair == i + 1, moved, self.total[r])
        for r in range(2):
            side_ref[side_rows(group, r), :] = self.total[r]


def emit(i, energy, cx, cy, gather, cross, chip):
    gather.put(i, energy, cx)
    stores = cross.put(mirrored(i), jnp.maximum(-cy[0], 0.0) * energy[0])
    return stores + chip.put(i, jnp.maximum(cy[1], 0.0) * energy[1])


def flush(stores):
    for ref, rows, value in stores:
        ref[rows, :] = value
    stores.clear()


def each_group(body):
    lax.fori_loop(0, LAST, lambda group, carry: body(group) or carry, 0)
    body(LAST)


def finish_packets(cross_ref, chip_ref):
    blank = jnp.zeros((SUB, LANES), F32)
    cross_ref[SPARE:PACKET, :] = blank
    chip_ref[SPARE:PACKET, :] = blank


def source_kernel(*refs):
    inputs, refs = refs[:8], refs[8:]
    e_ref, cross_ref, chip_ref, side_ref, fields_ref, raw = refs[:6]
    held, sems = refs[6:13], refs[13]
    odd, col, sign = position()
    copies = [
        pltpu.make_async_copy(source, target, sems.at[GROUPS + k])
        for k, (source, target) in enumerate(zip(inputs[1:], held))
    ]

    def chunk(group, size):
        rows = pl.ds(group * CHUNK, size)
        return pltpu.make_async_copy(inputs[0].at[rows], raw.at[rows], sems.at[group])

    final = chunk(LAST, TAIL * 2 * ND)
    for group in range(LAST):
        chunk(group, CHUNK).start()
    final.start()
    for copy in copies:
        copy.start()
    raw[NF * 2 * ND :, :] = jnp.zeros(((PADF - NF) * 2 * ND, LANES), F32)
    ws_ref, wd_ref, u_ref, v_ref, rx_ref, ry_ref, sea_ref = held

    def stats(group, sums):
        if group is LAST:
            final.wait()
        else:
            chunk(group, CHUNK).wait()
        s, j = radian_of(group)
        valid = j < NF
        w1 = jnp.where(valid, s * ((math.exp(RATIO) - 1.0) * DTH), 0.0)
        w2 = jnp.where(valid, (math.exp(RATIO) - 1.0) * DTH, 0.0)
        out = []
        for r in range(2):
            parts = [None, None, None, None]
            r_from = jnp.where(odd == 1, 1 - r, r)
            stores = []
            for i in range(ND):
                i_from = jnp.where(odd == 1, 2 * mirrored(i), 2 * i)
                got = raw[pl.ds(group * CHUNK + i_from + r_from, SUB, stride=2 * ND), :]
                stores.append((e_ref, field_rows(group, r, i), got))
                k = i % 4
                parts[k] = got if parts[k] is None else parts[k] + got
                if i % 9 == 8:
                    flush(stores)
            part = (parts[0] + parts[1]) + (parts[2] + parts[3])
            out.append((sums[r][0] + part * w1, sums[r][1] + part * w2))
        return tuple(out)

    blank = jnp.zeros((SUB, LANES), F32)
    sums = stats(LAST, lax.fori_loop(0, LAST, stats, ((blank, blank), (blank, blank))))
    for copy in copies:
        copy.wait()
    wind_x, wind_y, sea, decay, u, v = [], [], [], [], [], []
    for r in range(2):
        total = jnp.sum(sums[r][0], axis=0, keepdims=True)
        inverse = jnp.sum(sums[r][1], axis=0, keepdims=True)
        mean_sigma = total / inverse
        mean_k = mean_sigma * mean_sigma / gravity
        ratio = total * mean_k * mean_k / steep_ref
        decay.append(spread(source_seconds * break_coef * ratio * ratio / mean_sigma))
        strength = row_of(ws_ref, odd, r, None) * (wind_factor / gravity)
        angle = row_of(wd_ref, odd, r, None) * sign
        wind_x.append(spread(strength * jnp.cos(angle)))
        wind_y.append(spread(strength * jnp.sin(angle)))
        own = [
            row_of(sea_ref, odd, r, col),
            courant_cells * row_of(u_ref, odd, r, col),
            courant_cells * sign * row_of(v_ref, odd, r, col),
        ]
        for k in range(3):
            fields_ref[2 * k + r : 2 * k + r + 1, :] = own[k]
        sea.append(spread(own[0]))
        u.append(spread(own[1]))
        v.append(spread(own[2]))
        rx = row_of(rx_ref, odd, r, col)
        ry = sign * row_of(ry_ref, odd, r, col)
        for i in range(ND):
            at = TURN + r * ND + i
            fields_ref[at : at + 1, :] = SIN[i] * rx - COS[i] * ry
    lane = lane_ids()

    def source(group):
        s, _ = radian_of(group)
        fc = (courant_cells * gravity / 2.0) / s
        gain = s * (source_seconds * wind_coef)
        damp = [sea[r] / (1.0 + decay[r] * s * s) for r in range(2)]
        base = group_base(group)
        cross, chip = Sender(cross_ref, group, base), Sender(chip_ref, group, base)
        gather, stores = Gather(lane), []
        for i in range(ND):
            energy, cx, cy = [], [], []
            for r in range(2):
                rows = field_rows(group, r, i)
                align = wind_x[r] * COS[i] + wind_y[r] * SIN[i]
                growth = gain * jnp.maximum(s * align - 1.0, 0.0)
                new = e_ref[rows, :] * damp[r] * (1.0 + growth)
                stores.append((e_ref, rows, new))
                energy.append(new)
                cx.append(fc * COS[i] + u[r])
                cy.append(fc * SIN[i] + v[r])
            stores += emit(i, energy, cx, cy, gather, cross, chip)
            if i % BATCH == BATCH - 1:
                flush(stores)
        gather.finish(side_ref, group)

    each_group(source)
    finish_packets(cross_ref, chip_ref)


def transport_kernel(last, e_ref, cross_in, chip_in, west_in, east_in, fields_ref, *rest):
    if last:
        out_hbm, work, sems = rest
    else:
        out_ref, cross_ref, chip_ref, side_ref = rest
    odd, _, _ = position()
    sea, u, v = [[spread(fields_ref[2 * k + r : 2 * k + r + 1, :]) for r in range(2)] for k in range(3)]
    lane = lane_ids()
    odd_lane = lax.rem(lane, 2) == 1
    blank = jnp.zeros((SUB, LANES), F32)

    def substep(group):
        s, _ = radian_of(group)
        c = (gravity / 2.0) / s
        fc = courant_cells * c
        tc = (substep_seconds / DTH) * c
        base = group_base(group)
        border = []
        for r in range(2):
            rows = side_rows(group, r)
            border.append(
                jnp.where(odd_lane, west_in[rows, :], pltpu.roll(east_in[rows, :], LANES - 2, 1))
            )

        def turned(r, i):
            energy = e_ref[field_rows(group, r, i), :]
            at = TURN + r * ND + i
            speed = tc * spread(fields_ref[at : at + 1, :])
            return energy, jnp.maximum(speed, 0.0) * energy, jnp.minimum(speed, 0.0) * energy

        before = [turned(r, ND - 1)[1] for r in range(2)]
        first = [turned(r, 0) for r in range(2)]
        here = first
        gather, stores = Gather(lane), []
        if not last:
            cross, chip = Sender(cross_ref, group, base), Sender(chip_ref, group, base)
        for i in range(ND):
            after = [turned(r, i + 1) for r in range(2)] if i + 1 < ND else first
            cx = [fc * COS[i] + u[r] for r in range(2)]
            cy = [fc * SIN[i] + v[r] for r in range(2)]
            energy = [here[r][0] for r in range(2)]
            py = [jnp.maximum(cy[r], 0.0) * energy[r] for r in range(2)]
            my = [jnp.minimum(cy[r], 0.0) * energy[r] for r in range(2)]
            from_cross = fetch(cross_in, group, base, i)
            from_chip = fetch(chip_in, group, base, mirrored(i))
            in_y = [from_cross - my[1], py[0] + from_chip]
            new = []
            for r in range(2):
                px = jnp.maximum(cx[r], 0.0) * energy[r]
                mx = jnp.minimum(cx[r], 0.0) * energy[r]
                brought = pltpu.roll(border[r], (LANES - (2 * i + 1)) % LANES, 1)
                px_in = jnp.where(lane == 0, brought, pltpu.roll(px, 1, 1))
                mx_in = jnp.where(lane == LANES - 1, brought, pltpu.roll(mx, LANES - 1, 1))
                stay = energy[r] - (px - mx) - (py[r] - my[r]) - (here[r][1] - here[r][2])
                gained = (px_in - mx_in) + in_y[r] + (before[r] - after[r][2])
                new.append(sea[r] * (stay + gained))
            for r in range(2):
                if last:
                    i_to = jnp.where(odd == 1, 2 * mirrored(i), 2 * i)
                    r_to = jnp.where(odd == 1, 1 - r, r)
                    start = group * CHUNK + i_to + r_to
                    stores.append((work, pl.ds(start, SUB, stride=2 * ND), new[r]))
                else:
                    stores.append((out_ref, field_rows(group, r, i), new[r]))
            if not last:
                stores += emit(i, new, cx, cy, gather, cross, chip)
            if i % BATCH == BATCH - 1:
                flush(stores)
            before = [here[r][1] for r in range(2)]
            here = after
        if not last:
            gather.finish(side_ref, group)

        if last:
            chunk(group).start()

    def chunk(group):
        rows = pl.ds(group * CHUNK, TAIL * 2 * ND if group is LAST else CHUNK)
        return pltpu.make_async_copy(work.at[rows], out_hbm.at[rows], sems.at[group])

    each_group(substep)
    if last:
        for group in range(LAST):
            chunk(group).wait()
        chunk(LAST).wait()
    else:
        finish_packets(cross_ref, chip_ref)


VMEM = pl.BlockSpec(memory_space=pltpu.VMEM)
HBM = pl.BlockSpec(memory_space=pltpu.HBM)
PARAMS = pltpu.CompilerParams(vmem_limit_bytes=24 * 1024 * 1024)


def shape(rows):
    return jax.ShapeDtypeStruct((rows, LANES), F32)


def packets():
    return [shape(FIELD), shape(PACKET), shape(PACKET), shape(SIDE)]


def exchange(cross, chip, side):
    geo, spec = lax.axis_size("geo"), lax.axis_size("spec")
    links = [(k, k + 1) for k in range(1, geo - 1, 2)]
    cores = [(k, k + 1) for k in range(0, geo, 2)]
    east = [(k, k + 1) for k in range(spec - 1)]
    both = lambda pairs: pairs + [(b, a) for a, b in pairs]
    return (
        lax.ppermute(cross, "geo", both(links)),
        lax.ppermute(chip, "geo", both(cores)),
        lax.ppermute(side, "spec", east),
        lax.ppermute(side, "spec", [(b, a) for a, b in east]),
    )


def per_device(
    spectrum, wind_speed, wind_dir, current_u, current_v, refract_x, refract_y, land_mask
):
    rows = spectrum.shape[0] * spectrum.shape[1] * spectrum.shape[2]
    flat = spectrum.reshape(rows, LANES)
    inputs = [flat, wind_speed, wind_dir, current_u, current_v, refract_x, refract_y, land_mask]
    inputs = [pltpu.with_memory_space_constraint(value, pltpu.HBM) for value in inputs]
    energy, cross, chip, side, fields = pl.pallas_call(
        source_kernel,
        out_shape=packets() + [shape(FIELDS)],
        in_specs=[HBM] * len(inputs),
        out_specs=[VMEM] * 5,
        scratch_shapes=[pltpu.VMEM((PADF * 2 * ND, LANES), F32)]
        + [pltpu.VMEM(value.shape, value.dtype) for value in inputs[1:]]
        + [pltpu.SemaphoreType.DMA((GROUPS + len(inputs) - 1,))],
        compiler_params=PARAMS,
        name="source",
    )(*inputs)
    halo = exchange(cross, chip, side)
    energy, cross, chip, side = pl.pallas_call(
        functools.partial(transport_kernel, False),
        out_shape=packets(),
        in_specs=[VMEM] * 6,
        out_specs=[VMEM] * 4,
        compiler_params=PARAMS,
        name="first_substep",
    )(energy, *halo, fields)
    halo = exchange(cross, chip, side)
    out = pl.pallas_call(
        functools.partial(transport_kernel, True),
        out_shape=shape(rows),
        in_specs=[VMEM] * 6,
        out_specs=HBM,
        scratch_shapes=[
            pltpu.VMEM((PADF * 2 * ND, LANES), F32),
            pltpu.SemaphoreType.DMA((GROUPS,)),
        ],
        compiler_params=PARAMS,
        name="second_substep",
    )(energy, *halo, fields)
    return out.reshape(spectrum.shape)


def solution(mesh):
    in_specs = (
        P(None, None, "geo", "spec"),
        P("geo", "spec"),
        P("geo", "spec"),
        P("geo", None),
        P("geo", None),
        P("geo", None),
        P("geo", None),
        P("geo", None),
    )
    out_specs = P(None, None, "geo", "spec")
    return jax.shard_map(
        per_device, mesh=mesh, in_specs=in_specs, out_specs=out_specs, check_vma=False
    )
```

```python
import functools
import math

import jax
import jax.numpy as jnp
from jax import lax
from jax.experimental import pallas as pl
from jax.experimental.pallas import tpu as pltpu
from jax.sharding import PartitionSpec as P

gravity = 9.81
lowest_radian = 2.0 * math.pi * 0.0373
log_span = 49.0 * math.log(1.1)
wind_coef = 1.7e-06
break_coef = 2.5e-05
steep_ref = 480.0
wind_factor = 1.1
source_seconds = 360.0
courant_cells = 0.02
substep_seconds = 180.0

NF = 50
ND = 36
LANES = 128
SUB = 8
GROUPS = 7
PADF = SUB * GROUPS
RATIO = log_span / (NF - 1)
DTH = 2.0 * math.pi / ND
COS = [math.cos(DTH * i) for i in range(ND)]
SIN = [math.sin(DTH * i) for i in range(ND)]
GSPEED = [gravity / (2.0 * lowest_radian * math.exp(RATIO * j)) for j in range(NF)]
FIRST = [
    min(j for j in range(NF) if GSPEED[j] * SIN[i] > -1.001) // SUB for i in range(ND)
]
RANK = [0] * ND
for place, i_of in enumerate(sorted(range(ND), key=lambda i: (FIRST[i], i))):
    RANK[i_of] = place
COUNT = [sum(1 for i in range(ND) if FIRST[i] <= g) for g in range(GROUPS)]
BASE = [SUB * sum(COUNT[:g]) for g in range(GROUPS)]
TAIL = NF - SUB * (GROUPS - 1)
FIT = SUB // TAIL
SPARE = BASE[-1] + SUB * (ND // FIT)
PACKET = SPARE + SUB
TURN = 8
FIELDS = TURN + 2 * ND
BATCH = 3
CHUNK = SUB * 2 * ND
FIELD = 2 * ND * PADF
SIDE = 2 * PADF
F32 = jnp.float32


def mirrored(i):
    return (ND - i) % ND


LAST = GROUPS - 1


def group_base(group):
    if group is LAST:
        return BASE[-1]
    total = 0
    for g in range(GROUPS - 1):
        total = total + jnp.where(group > g, SUB * COUNT[g], 0)
    return total


def slot(base, group, i):
    place = base + SUB * RANK[i]
    if FIRST[i] > 0:
        place = jnp.where(group >= FIRST[i], place, SPARE)
    return aligned(place)


def aligned(start):
    return pl.ds(start if isinstance(start, int) else pl.multiple_of(start, SUB), SUB)


def field_rows(group, r, i):
    return aligned((r * ND + i) * PADF + group * SUB)


def side_rows(group, r):
    return aligned(r * PADF + group * SUB)


def fetch(ref, group, base, i):
    if group is LAST:
        got = ref[aligned(BASE[-1] + SUB * (RANK[i] // FIT)), :]
        return pltpu.roll(got, (SUB - TAIL * (RANK[i] % FIT)) % SUB, 0)
    return ref[slot(base, group, i), :]


class Sender:
    def __init__(self, ref, group, base):
        self.ref, self.group, self.base, self.shared = ref, group, base, {}

    def put(self, i, value):
        if self.group is not LAST:
            return [(self.ref, slot(self.base, self.group, i), value)]
        block, part = RANK[i] // FIT, RANK[i] % FIT
        held = self.shared.setdefault(block, {})
        held[part] = pltpu.roll(value, TAIL * part, 0) if part else value
        if len(held) < FIT:
            return []
        place = lax.broadcasted_iota(jnp.int32, (SUB, LANES), 0)
        full = held[FIT - 1]
        for part in range(FIT - 1):
            inside = (place >= TAIL * part) & (place < TAIL * (part + 1))
            full = jnp.where(inside, held[part], full)
        return [(self.ref, aligned(BASE[-1] + SUB * block), full)]


def radian_of(group):
    j = lax.broadcasted_iota(jnp.int32, (SUB, LANES), 0) + group * SUB
    return lowest_radian * jnp.exp(j.astype(F32) * RATIO), j


def position():
    odd = lax.rem(lax.axis_index("geo"), 2)
    col = pl.multiple_of(lax.axis_index("spec") * LANES, LANES)
    sign = jnp.where(odd == 1, -1.0, 1.0).astype(F32)
    return odd, col, sign


def inside():
    geo, spec = lax.axis_index("geo"), lax.axis_index("spec")
    first, last = lax.axis_size("geo") - 1, lax.axis_size("spec") - 1
    keep = lambda edge: jnp.where(edge, 0.0, 1.0).astype(F32)
    return keep((geo == 0) | (geo == first)), keep(spec == 0), keep(spec == last)


def row_of(ref, odd, r, col):
    window = (ref[...] if col is None else ref[:, pl.ds(col, LANES)]).astype(F32)
    first, second = window[0:1], window[1:2]
    own, other = (first, second) if r == 0 else (second, first)
    return jnp.where(odd == 1, other, own)


def spread(row):
    return jnp.broadcast_to(row, (SUB, LANES))


def lane_ids():
    return lax.broadcasted_iota(jnp.int32, (SUB, LANES), 1)


class Gather:
    def __init__(self, lane):
        self.lane, self.pair = lane, lax.shift_right_logical(lane + 1, 1)
        self.total = [jnp.zeros((SUB, LANES), F32)] * 2
        self.queue = []

    def put(self, i, energy, cx):
        flux = []
        for r in range(2):
            speed = jnp.where(self.lane == 0, jnp.minimum(cx[r], 0.0), jnp.maximum(cx[r], 0.0))
            flux.append(speed * energy[r])
        self.queue.append((i, flux))

    def finish(self, side_ref, group):
        for i, flux in self.queue:
            for r in range(2):
                moved = pltpu.roll(flux[r], 2 * i + 2, 1)
                self.total[r] = jnp.where(self.pair == i + 1, moved, self.total[r])
        for r in range(2):
            side_ref[side_rows(group, r), :] = self.total[r]


def emit(i, energy, cx, cy, gather, cross, chip):
    gather.put(i, energy, cx)
    stores = cross.put(mirrored(i), jnp.maximum(-cy[0], 0.0) * energy[0])
    return stores + chip.put(i, jnp.maximum(cy[1], 0.0) * energy[1])


def flush(stores):
    for ref, rows, value in stores:
        ref[rows, :] = value
    stores.clear()


def each_group(body):
    lax.fori_loop(0, LAST, lambda group, carry: body(group) or carry, 0)
    body(LAST)


def finish_packets(cross_ref, chip_ref):
    blank = jnp.zeros((SUB, LANES), F32)
    cross_ref[SPARE:PACKET, :] = blank
    chip_ref[SPARE:PACKET, :] = blank


def source_kernel(*refs):
    inputs, refs = refs[:8], refs[8:]
    e_ref, cross_ref, chip_ref, side_ref, fields_ref, raw = refs[:6]
    held, sems = refs[6:13], refs[13]
    odd, col, sign = position()
    copies = [
        pltpu.make_async_copy(source, target, sems.at[GROUPS + k])
        for k, (source, target) in enumerate(zip(inputs[1:], held))
    ]

    def chunk(group, size):
        rows = pl.ds(group * CHUNK, size)
        return pltpu.make_async_copy(inputs[0].at[rows], raw.at[rows], sems.at[group])

    final = chunk(LAST, TAIL * 2 * ND)
    for group in range(LAST):
        chunk(group, CHUNK).start()
    final.start()
    for copy in copies:
        copy.start()
    raw[NF * 2 * ND :, :] = jnp.zeros(((PADF - NF) * 2 * ND, LANES), F32)
    ws_ref, wd_ref, u_ref, v_ref, rx_ref, ry_ref, sea_ref = held

    def stats(group, sums):
        if group is LAST:
            final.wait()
        else:
            chunk(group, CHUNK).wait()
        s, j = radian_of(group)
        valid = j < NF
        w1 = jnp.where(valid, s * ((math.exp(RATIO) - 1.0) * DTH), 0.0)
        w2 = jnp.where(valid, (math.exp(RATIO) - 1.0) * DTH, 0.0)
        out = []
        for r in range(2):
            parts = [None, None, None, None]
            r_from = jnp.where(odd == 1, 1 - r, r)
            stores = []
            for i in range(ND):
                i_from = jnp.where(odd == 1, 2 * mirrored(i), 2 * i)
                got = raw[pl.ds(group * CHUNK + i_from + r_from, SUB, stride=2 * ND), :]
                stores.append((e_ref, field_rows(group, r, i), got))
                k = i % 4
                parts[k] = got if parts[k] is None else parts[k] + got
                if i % 9 == 8:
                    flush(stores)
            part = (parts[0] + parts[1]) + (parts[2] + parts[3])
            out.append((sums[r][0] + part * w1, sums[r][1] + part * w2))
        return tuple(out)

    blank = jnp.zeros((SUB, LANES), F32)
    sums = stats(LAST, lax.fori_loop(0, LAST, stats, ((blank, blank), (blank, blank))))
    for copy in copies:
        copy.wait()
    wind_x, wind_y, sea, decay, u, v = [], [], [], [], [], []
    for r in range(2):
        total = jnp.sum(sums[r][0], axis=0, keepdims=True)
        inverse = jnp.sum(sums[r][1], axis=0, keepdims=True)
        mean_sigma = total / inverse
        mean_k = mean_sigma * mean_sigma / gravity
        ratio = total * mean_k * mean_k / steep_ref
        decay.append(spread(source_seconds * break_coef * ratio * ratio / mean_sigma))
        strength = row_of(ws_ref, odd, r, None) * (wind_factor / gravity)
        angle = row_of(wd_ref, odd, r, None) * sign
        wind_x.append(spread(strength * jnp.cos(angle)))
        wind_y.append(spread(strength * jnp.sin(angle)))
        own = [
            row_of(sea_ref, odd, r, col),
            courant_cells * row_of(u_ref, odd, r, col),
            courant_cells * sign * row_of(v_ref, odd, r, col),
        ]
        for k in range(3):
            fields_ref[2 * k + r : 2 * k + r + 1, :] = own[k]
        sea.append(spread(own[0]))
        u.append(spread(own[1]))
        v.append(spread(own[2]))
        rx = row_of(rx_ref, odd, r, col)
        ry = sign * row_of(ry_ref, odd, r, col)
        for i in range(ND):
            at = TURN + r * ND + i
            fields_ref[at : at + 1, :] = SIN[i] * rx - COS[i] * ry
    lane = lane_ids()

    def source(group):
        s, _ = radian_of(group)
        fc = (courant_cells * gravity / 2.0) / s
        gain = s * (source_seconds * wind_coef)
        damp = [sea[r] / (1.0 + decay[r] * s * s) for r in range(2)]
        base = group_base(group)
        cross, chip = Sender(cross_ref, group, base), Sender(chip_ref, group, base)
        gather, stores = Gather(lane), []
        for i in range(ND):
            energy, cx, cy = [], [], []
            for r in range(2):
                rows = field_rows(group, r, i)
                align = wind_x[r] * COS[i] + wind_y[r] * SIN[i]
                growth = gain * jnp.maximum(s * align - 1.0, 0.0)
                new = e_ref[rows, :] * damp[r] * (1.0 + growth)
                stores.append((e_ref, rows, new))
                energy.append(new)
                cx.append(fc * COS[i] + u[r])
                cy.append(fc * SIN[i] + v[r])
            stores += emit(i, energy, cx, cy, gather, cross, chip)
            if i % BATCH == BATCH - 1:
                flush(stores)
        gather.finish(side_ref, group)

    each_group(source)
    finish_packets(cross_ref, chip_ref)


def transport_kernel(last, e_ref, cross_in, chip_in, west_in, east_in, fields_ref, *rest):
    if last:
        out_hbm, work, sems = rest
    else:
        out_ref, cross_ref, chip_ref, side_ref = rest
    odd, _, _ = position()
    keep_cross, keep_west, keep_east = inside()
    sea, u, v = [[spread(fields_ref[2 * k + r : 2 * k + r + 1, :]) for r in range(2)] for k in range(3)]
    lane = lane_ids()
    odd_lane = lax.rem(lane, 2) == 1
    blank = jnp.zeros((SUB, LANES), F32)

    def substep(group):
        s, _ = radian_of(group)
        c = (gravity / 2.0) / s
        fc = courant_cells * c
        tc = (substep_seconds / DTH) * c
        base = group_base(group)
        border = []
        for r in range(2):
            rows = side_rows(group, r)
            from_west = keep_west * west_in[rows, :]
            from_east = pltpu.roll(keep_east * east_in[rows, :], LANES - 2, 1)
            border.append(jnp.where(odd_lane, from_west, from_east))

        def turned(r, i):
            energy = e_ref[field_rows(group, r, i), :]
            at = TURN + r * ND + i
            speed = tc * spread(fields_ref[at : at + 1, :])
            return energy, jnp.maximum(speed, 0.0) * energy, jnp.minimum(speed, 0.0) * energy

        before = [turned(r, ND - 1)[1] for r in range(2)]
        first = [turned(r, 0) for r in range(2)]
        here = first
        gather, stores = Gather(lane), []
        if not last:
            cross, chip = Sender(cross_ref, group, base), Sender(chip_ref, group, base)
        for i in range(ND):
            after = [turned(r, i + 1) for r in range(2)] if i + 1 < ND else first
            cx = [fc * COS[i] + u[r] for r in range(2)]
            cy = [fc * SIN[i] + v[r] for r in range(2)]
            energy = [here[r][0] for r in range(2)]
            py = [jnp.maximum(cy[r], 0.0) * energy[r] for r in range(2)]
            my = [jnp.minimum(cy[r], 0.0) * energy[r] for r in range(2)]
            from_cross = keep_cross * fetch(cross_in, group, base, i)
            from_chip = fetch(chip_in, group, base, mirrored(i))
            in_y = [from_cross - my[1], py[0] + from_chip]
            new = []
            for r in range(2):
                px = jnp.maximum(cx[r], 0.0) * energy[r]
                mx = jnp.minimum(cx[r], 0.0) * energy[r]
                brought = pltpu.roll(border[r], (LANES - (2 * i + 1)) % LANES, 1)
                px_in = jnp.where(lane == 0, brought, pltpu.roll(px, 1, 1))
                mx_in = jnp.where(lane == LANES - 1, brought, pltpu.roll(mx, LANES - 1, 1))
                stay = energy[r] - (px - mx) - (py[r] - my[r]) - (here[r][1] - here[r][2])
                gained = (px_in - mx_in) + in_y[r] + (before[r] - after[r][2])
                new.append(sea[r] * (stay + gained))
            for r in range(2):
                if last:
                    i_to = jnp.where(odd == 1, 2 * mirrored(i), 2 * i)
                    r_to = jnp.where(odd == 1, 1 - r, r)
                    start = group * CHUNK + i_to + r_to
                    stores.append((work, pl.ds(start, SUB, stride=2 * ND), new[r]))
                else:
                    stores.append((out_ref, field_rows(group, r, i), new[r]))
            if not last:
                stores += emit(i, new, cx, cy, gather, cross, chip)
            if i % BATCH == BATCH - 1:
                flush(stores)
            before = [here[r][1] for r in range(2)]
            here = after
        if not last:
            gather.finish(side_ref, group)

        if last:
            chunk(group).start()

    def chunk(group):
        rows = pl.ds(group * CHUNK, TAIL * 2 * ND if group is LAST else CHUNK)
        return pltpu.make_async_copy(work.at[rows], out_hbm.at[rows], sems.at[group])

    each_group(substep)
    if last:
        for group in range(LAST):
            chunk(group).wait()
        chunk(LAST).wait()
    else:
        finish_packets(cross_ref, chip_ref)


VMEM = pl.BlockSpec(memory_space=pltpu.VMEM)
HBM = pl.BlockSpec(memory_space=pltpu.HBM)
PARAMS = pltpu.CompilerParams(vmem_limit_bytes=24 * 1024 * 1024)


def shape(rows):
    return jax.ShapeDtypeStruct((rows, LANES), F32)


def packets():
    return [shape(FIELD), shape(PACKET), shape(PACKET), shape(SIDE)]


def exchange(cross, chip, side):
    geo, spec = lax.axis_size("geo"), lax.axis_size("spec")
    place = lambda row, col: row * spec + col
    links = [(place(k, c), place(k + 1, c)) for k in range(1, geo - 1, 2) for c in range(spec)]
    links += [(place(k, c), place(k, c + 1)) for k in (0, geo - 1) for c in range(0, spec, 2)]
    cores = [(k, k + 1) for k in range(0, geo, 2)]
    east = [(k, (k + 1) % spec) for k in range(spec)]
    both = lambda pairs: pairs + [(b, a) for a, b in pairs]
    return (
        lax.ppermute(cross, ("geo", "spec"), both(links)),
        lax.ppermute(chip, "geo", both(cores)),
        lax.ppermute(side, "spec", east),
        lax.ppermute(side, "spec", [(b, a) for a, b in east]),
    )


def per_device(
    spectrum, wind_speed, wind_dir, current_u, current_v, refract_x, refract_y, land_mask
):
    rows = spectrum.shape[0] * spectrum.shape[1] * spectrum.shape[2]
    flat = spectrum.reshape(rows, LANES)
    inputs = [flat, wind_speed, wind_dir, current_u, current_v, refract_x, refract_y, land_mask]
    inputs = [pltpu.with_memory_space_constraint(value, pltpu.HBM) for value in inputs]
    energy, cross, chip, side, fields = pl.pallas_call(
        source_kernel,
        out_shape=packets() + [shape(FIELDS)],
        in_specs=[HBM] * len(inputs),
        out_specs=[VMEM] * 5,
        scratch_shapes=[pltpu.VMEM((PADF * 2 * ND, LANES), F32)]
        + [pltpu.VMEM(value.shape, value.dtype) for value in inputs[1:]]
        + [pltpu.SemaphoreType.DMA((GROUPS + len(inputs) - 1,))],
        compiler_params=PARAMS,
        name="source",
    )(*inputs)
    halo = exchange(cross, chip, side)
    energy, cross, chip, side = pl.pallas_call(
        functools.partial(transport_kernel, False),
        out_shape=packets(),
        in_specs=[VMEM] * 6,
        out_specs=[VMEM] * 4,
        compiler_params=PARAMS,
        name="first_substep",
    )(energy, *halo, fields)
    halo = exchange(cross, chip, side)
    out = pl.pallas_call(
        functools.partial(transport_kernel, True),
        out_shape=shape(rows),
        in_specs=[VMEM] * 6,
        out_specs=HBM,
        scratch_shapes=[
            pltpu.VMEM((PADF * 2 * ND, LANES), F32),
            pltpu.SemaphoreType.DMA((GROUPS,)),
        ],
        compiler_params=PARAMS,
        name="second_substep",
    )(energy, *halo, fields)
    return out.reshape(spectrum.shape)


def solution(mesh):
    in_specs = (
        P(None, None, "geo", "spec"),
        P("geo", "spec"),
        P("geo", "spec"),
        P("geo", None),
        P("geo", None),
        P("geo", None),
        P("geo", None),
        P("geo", None),
    )
    out_specs = P(None, None, "geo", "spec")
    return jax.shard_map(
        per_device, mesh=mesh, in_specs=in_specs, out_specs=out_specs, check_vma=False
    )
```

```python
import functools
import math

import jax
import jax.numpy as jnp
from jax import lax
from jax.experimental import pallas as pl
from jax.experimental.pallas import tpu as pltpu
from jax.sharding import PartitionSpec as P

gravity = 9.81
lowest_radian = 2.0 * math.pi * 0.0373
log_span = 49.0 * math.log(1.1)
wind_coef = 1.7e-06
break_coef = 2.5e-05
steep_ref = 480.0
wind_factor = 1.1
source_seconds = 360.0
courant_cells = 0.02
substep_seconds = 180.0

NF = 50
ND = 36
LANES = 128
SUB = 8
GROUPS = 7
PADF = SUB * GROUPS
RATIO = log_span / (NF - 1)
DTH = 2.0 * math.pi / ND
COS = [math.cos(DTH * i) for i in range(ND)]
SIN = [math.sin(DTH * i) for i in range(ND)]
GSPEED = [gravity / (2.0 * lowest_radian * math.exp(RATIO * j)) for j in range(NF)]
FIRST = [
    min(j for j in range(NF) if GSPEED[j] * SIN[i] > -1.001) // SUB for i in range(ND)
]
RANK = [0] * ND
for place, i_of in enumerate(sorted(range(ND), key=lambda i: (FIRST[i], i))):
    RANK[i_of] = place
COUNT = [sum(1 for i in range(ND) if FIRST[i] <= g) for g in range(GROUPS)]
BASE = [SUB * sum(COUNT[:g]) for g in range(GROUPS)]
TAIL = NF - SUB * (GROUPS - 1)
FIT = SUB // TAIL
SPARE = BASE[-1] + SUB * (ND // FIT)
PACKET = SPARE + SUB
TURN = 8
FIELDS = TURN + 2 * ND
BATCH = 3
SPAN = 2 * 10**10
CHUNK = SUB * 2 * ND
FIELD = 2 * ND * PADF
SIDE = 2 * PADF
F32 = jnp.float32


def mirrored(i):
    return (ND - i) % ND


LAST = GROUPS - 1


def group_base(group):
    if group is LAST:
        return BASE[-1]
    total = 0
    for g in range(GROUPS - 1):
        total = total + jnp.where(group > g, SUB * COUNT[g], 0)
    return total


def slot(base, group, i):
    place = base + SUB * RANK[i]
    if FIRST[i] > 0:
        place = jnp.where(group >= FIRST[i], place, SPARE)
    return aligned(place)


def aligned(start):
    return pl.ds(start if isinstance(start, int) else pl.multiple_of(start, SUB), SUB)


def field_rows(group, r, i):
    return aligned((r * ND + i) * PADF + group * SUB)


def side_rows(group, r):
    return aligned(r * PADF + group * SUB)


def fetch(ref, group, base, i):
    if group is LAST:
        got = ref[aligned(BASE[-1] + SUB * (RANK[i] // FIT)), :]
        return pltpu.roll(got, (SUB - TAIL * (RANK[i] % FIT)) % SUB, 0)
    return ref[slot(base, group, i), :]


class Sender:
    def __init__(self, ref, group, base):
        self.ref, self.group, self.base, self.shared = ref, group, base, {}

    def put(self, i, value):
        if self.group is not LAST:
            return [(self.ref, slot(self.base, self.group, i), value)]
        block, part = RANK[i] // FIT, RANK[i] % FIT
        held = self.shared.setdefault(block, {})
        held[part] = pltpu.roll(value, TAIL * part, 0) if part else value
        if len(held) < FIT:
            return []
        place = lax.broadcasted_iota(jnp.int32, (SUB, LANES), 0)
        full = held[FIT - 1]
        for part in range(FIT - 1):
            inside = (place >= TAIL * part) & (place < TAIL * (part + 1))
            full = jnp.where(inside, held[part], full)
        return [(self.ref, aligned(BASE[-1] + SUB * block), full)]


def radian_of(group):
    j = lax.broadcasted_iota(jnp.int32, (SUB, LANES), 0) + group * SUB
    return lowest_radian * jnp.exp(j.astype(F32) * RATIO), j


def position():
    odd = lax.rem(lax.axis_index("geo"), 2)
    col = pl.multiple_of(lax.axis_index("spec") * LANES, LANES)
    sign = jnp.where(odd == 1, -1.0, 1.0).astype(F32)
    return odd, col, sign


def inside():
    geo, spec = lax.axis_index("geo"), lax.axis_index("spec")
    first, last = lax.axis_size("geo") - 1, lax.axis_size("spec") - 1
    keep = lambda edge: jnp.where(edge, 0.0, 1.0).astype(F32)
    return keep((geo == 0) | (geo == first)), keep(spec == 0), keep(spec == last)


def row_of(ref, odd, r, col):
    window = (ref[...] if col is None else ref[:, pl.ds(col, LANES)]).astype(F32)
    first, second = window[0:1], window[1:2]
    own, other = (first, second) if r == 0 else (second, first)
    return jnp.where(odd == 1, other, own)


def spread(row):
    return jnp.broadcast_to(row, (SUB, LANES))


def lane_ids():
    return lax.broadcasted_iota(jnp.int32, (SUB, LANES), 1)


class Gather:
    def __init__(self, lane):
        self.lane, self.pair = lane, lax.shift_right_logical(lane + 1, 1)
        self.total = [jnp.zeros((SUB, LANES), F32)] * 2
        self.queue = []

    def put(self, i, energy, cx):
        flux = []
        for r in range(2):
            speed = jnp.where(self.lane == 0, jnp.minimum(cx[r], 0.0), jnp.maximum(cx[r], 0.0))
            flux.append(speed * energy[r])
        self.queue.append((i, flux))

    def finish(self, side_ref, group):
        for i, flux in self.queue:
            for r in range(2):
                moved = pltpu.roll(flux[r], 2 * i + 2, 1)
                self.total[r] = jnp.where(self.pair == i + 1, moved, self.total[r])
        for r in range(2):
            side_ref[side_rows(group, r), :] = self.total[r]


def cross_flux(cy, energy):
    return jnp.maximum(-cy, 0.0) * energy


def chip_flux(cy, energy):
    return jnp.maximum(cy, 0.0) * energy


def flush(stores):
    for ref, rows, value in stores:
        ref[rows, :] = value
    stores.clear()


def each_group(body):
    lax.fori_loop(0, LAST, lambda group, carry: body(group) or carry, 0)
    body(LAST)


def finish_packet(ref):
    ref[SPARE:PACKET, :] = jnp.zeros((SUB, LANES), F32)


def field_of(fields_ref, kind):
    return [spread(fields_ref[2 * kind + r : 2 * kind + r + 1, :]) for r in range(2)]


def source_kernel(*refs):
    inputs, refs = refs[:8], refs[8:]
    e_ref, cross_ref, side_ref, fields_ref, raw = refs[:5]
    held, sems = refs[5:12], refs[12]
    odd, col, sign = position()
    copies = [
        pltpu.make_async_copy(source, target, sems.at[GROUPS + k])
        for k, (source, target) in enumerate(zip(inputs[1:], held))
    ]

    def chunk(group, size):
        rows = pl.ds(group * CHUNK, size)
        return pltpu.make_async_copy(inputs[0].at[rows], raw.at[rows], sems.at[group])

    final = chunk(LAST, TAIL * 2 * ND)
    for group in range(LAST):
        chunk(group, CHUNK).start()
    final.start()
    for copy in copies:
        copy.start()
    raw[NF * 2 * ND :, :] = jnp.zeros(((PADF - NF) * 2 * ND, LANES), F32)
    ws_ref, wd_ref, u_ref, v_ref, rx_ref, ry_ref, sea_ref = held

    def stats(group, sums):
        if group is LAST:
            final.wait()
        else:
            chunk(group, CHUNK).wait()
        s, j = radian_of(group)
        valid = j < NF
        w1 = jnp.where(valid, s * ((math.exp(RATIO) - 1.0) * DTH), 0.0)
        w2 = jnp.where(valid, (math.exp(RATIO) - 1.0) * DTH, 0.0)
        out = []
        for r in range(2):
            parts = [None, None, None, None]
            r_from = jnp.where(odd == 1, 1 - r, r)
            stores = []
            for i in range(ND):
                i_from = jnp.where(odd == 1, 2 * mirrored(i), 2 * i)
                got = raw[pl.ds(group * CHUNK + i_from + r_from, SUB, stride=2 * ND), :]
                stores.append((e_ref, field_rows(group, r, i), got))
                k = i % 4
                parts[k] = got if parts[k] is None else parts[k] + got
                if i % 9 == 8:
                    flush(stores)
            part = (parts[0] + parts[1]) + (parts[2] + parts[3])
            out.append((sums[r][0] + part * w1, sums[r][1] + part * w2))
        return tuple(out)

    blank = jnp.zeros((SUB, LANES), F32)
    sums = stats(LAST, lax.fori_loop(0, LAST, stats, ((blank, blank), (blank, blank))))
    for copy in copies:
        copy.wait()
    wind_x, wind_y, sea, decay, u = [], [], [], [], []
    for r in range(2):
        total = jnp.sum(sums[r][0], axis=0, keepdims=True)
        inverse = jnp.sum(sums[r][1], axis=0, keepdims=True)
        mean_sigma = total / inverse
        mean_k = mean_sigma * mean_sigma / gravity
        ratio = total * mean_k * mean_k / steep_ref
        decay.append(spread(source_seconds * break_coef * ratio * ratio / mean_sigma))
        strength = row_of(ws_ref, odd, r, None) * (wind_factor / gravity)
        angle = row_of(wd_ref, odd, r, None) * sign
        wind_x.append(spread(strength * jnp.cos(angle)))
        wind_y.append(spread(strength * jnp.sin(angle)))
        own = [
            row_of(sea_ref, odd, r, col),
            courant_cells * row_of(u_ref, odd, r, col),
            courant_cells * sign * row_of(v_ref, odd, r, col),
        ]
        for k in range(3):
            fields_ref[2 * k + r : 2 * k + r + 1, :] = own[k]
        sea.append(spread(own[0]))
        u.append(spread(own[1]))
        if r == 0:
            v = spread(own[2])
        rx = row_of(rx_ref, odd, r, col)
        ry = sign * row_of(ry_ref, odd, r, col)
        for i in range(ND):
            at = TURN + r * ND + i
            fields_ref[at : at + 1, :] = SIN[i] * rx - COS[i] * ry
    lane = lane_ids()

    def source(group):
        s, _ = radian_of(group)
        fc = (courant_cells * gravity / 2.0) / s
        gain = s * (source_seconds * wind_coef)
        damp = [sea[r] / (1.0 + decay[r] * s * s) for r in range(2)]
        base = group_base(group)
        cross = Sender(cross_ref, group, base)
        gather, stores = Gather(lane), []
        for i in range(ND):
            energy, cx = [], []
            for r in range(2):
                rows = field_rows(group, r, i)
                align = wind_x[r] * COS[i] + wind_y[r] * SIN[i]
                growth = gain * jnp.maximum(s * align - 1.0, 0.0)
                new = e_ref[rows, :] * damp[r] * (1.0 + growth)
                stores.append((e_ref, rows, new))
                energy.append(new)
                cx.append(fc * COS[i] + u[r])
            gather.put(i, energy, cx)
            stores += cross.put(mirrored(i), cross_flux(fc * SIN[i] + v, energy[0]))
            if i % BATCH == BATCH - 1:
                flush(stores)
        gather.finish(side_ref, group)

    each_group(source)
    finish_packet(cross_ref)


def borders(group, sides, keep_west, keep_east, sign):
    odd_lane = lax.rem(lane_ids(), 2) == 1
    even_col = lax.rem(lax.axis_index("spec"), 2) == 0
    out = []
    for r in range(2):
        first, second = [ref[side_rows(group, r), :] for ref in sides]
        from_west = keep_west * jnp.where(even_col, second, first)
        from_east = (sign * keep_east) * jnp.where(even_col, first, second)
        from_east = pltpu.roll(from_east, LANES - 2, 1)
        out.append(jnp.where(odd_lane, from_west, from_east))
    return out


def brought(border, i):
    return pltpu.roll(border, (LANES - (2 * i + 1)) % LANES, 1)


def speeds(group):
    s, _ = radian_of(group)
    c = (gravity / 2.0) / s
    return courant_cells * c, (substep_seconds / DTH) * c


def transport_kernel(first_step, *refs):
    if first_step:
        e_ref, *sides, fields_ref, out_ref, cross_ref, chip_ref = refs
    else:
        e_ref, fields_ref, out_ref = refs
    _, keep_west, keep_east = inside()
    sea, u, v = [field_of(fields_ref, kind) for kind in range(3)]
    lane = lane_ids()

    def substep(group):
        fc, tc = speeds(group)
        if first_step:
            base = group_base(group)
            border = borders(group, sides, keep_west, keep_east, 1.0)
            cross, chip = Sender(cross_ref, group, base), Sender(chip_ref, group, base)

        def turned(r, i):
            energy = e_ref[field_rows(group, r, i), :]
            at = TURN + r * ND + i
            speed = tc * spread(fields_ref[at : at + 1, :])
            return energy, jnp.maximum(speed, 0.0) * energy, jnp.minimum(speed, 0.0) * energy

        before = [turned(r, ND - 1)[1] for r in range(2)]
        first = [turned(r, 0) for r in range(2)]
        here = first
        stores = []
        for i in range(ND):
            after = [turned(r, i + 1) for r in range(2)] if i + 1 < ND else first
            cx = [fc * COS[i] + u[r] for r in range(2)]
            cy = [fc * SIN[i] + v[r] for r in range(2)]
            energy = [here[r][0] for r in range(2)]
            py = [jnp.maximum(cy[r], 0.0) * energy[r] for r in range(2)]
            my = [jnp.minimum(cy[r], 0.0) * energy[r] for r in range(2)]
            in_y = [-my[1], py[0]]
            new = []
            for r in range(2):
                px = jnp.maximum(cx[r], 0.0) * energy[r]
                mx = jnp.minimum(cx[r], 0.0) * energy[r]
                edge = brought(border[r], i) if first_step else 0.0
                px_in = jnp.where(lane == 0, edge, pltpu.roll(px, 1, 1))
                mx_in = jnp.where(lane == LANES - 1, edge, pltpu.roll(mx, LANES - 1, 1))
                stay = energy[r] - (px - mx) - (py[r] - my[r]) - (here[r][1] - here[r][2])
                gained = (px_in - mx_in) + in_y[r] + (before[r] - after[r][2])
                new.append(sea[r] * (stay + gained))
            for r in range(2):
                stores.append((out_ref, field_rows(group, r, i), new[r]))
            if first_step:
                stores += cross.put(mirrored(i), cross_flux(cy[0], new[0]))
                stores += chip.put(i, py[1])
            if i % BATCH == BATCH - 1:
                flush(stores)
            before = [here[r][1] for r in range(2)]
            here = after

    each_group(substep)
    if first_step:
        finish_packet(cross_ref)
        finish_packet(chip_ref)
        cross_ref[PACKET:, :] = jnp.zeros((SUB, LANES), F32)
        cross_ref[PACKET : PACKET + 1, :] = fields_ref[0:1, :]
        cross_ref[PACKET + 1 : PACKET + 2, :] = fields_ref[4:5, :]


def complete_kernel(part_ref, cross_in, chip_in, fields_ref, e_ref, chip_ref, side_ref):
    keep_cross, _, _ = inside()
    sea, u, v = [field_of(fields_ref, kind) for kind in range(3)]
    sea_cross = keep_cross * sea[0]
    lane = lane_ids()

    def complete(group):
        fc, _ = speeds(group)
        base = group_base(group)
        chip, gather, stores = Sender(chip_ref, group, base), Gather(lane), []
        for i in range(ND):
            rows = [field_rows(group, r, i) for r in range(2)]
            new = [
                part_ref[rows[0], :] + sea_cross * fetch(cross_in, group, base, i),
                part_ref[rows[1], :] + sea[1] * fetch(chip_in, group, base, mirrored(i)),
            ]
            gather.put(i, new, [fc * COS[i] + u[r] for r in range(2)])
            for r in range(2):
                stores.append((e_ref, rows[r], new[r]))
            stores += chip.put(i, chip_flux(fc * SIN[i] + v[1], new[1]))
            if i % BATCH == BATCH - 1:
                flush(stores)
        gather.finish(side_ref, group)

    each_group(complete)
    finish_packet(chip_ref)


def finish_kernel(
    part_ref, sent_ref, cross_in, chip_in, side_a, side_b, fields_ref, out_hbm, work, sems
):
    odd, _, _ = position()
    keep_cross, keep_west, keep_east = inside()
    sea = field_of(fields_ref, 0)
    sea_cross = keep_cross * sea[0]
    their_sea = spread(cross_in[PACKET : PACKET + 1, :])
    their_v = spread(cross_in[PACKET + 1 : PACKET + 2, :])
    lane = lane_ids()
    rim = jnp.where((lane == 0) | (lane == LANES - 1), 1.0, 0.0)
    sea_rim = [sea[r] * rim for r in range(2)]

    def chunk(group):
        rows = pl.ds(group * CHUNK, TAIL * 2 * ND if group is LAST else CHUNK)
        return pltpu.make_async_copy(work.at[rows], out_hbm.at[rows], sems.at[group])

    def finish(group):
        fc, _ = speeds(group)
        base = group_base(group)
        border = borders(group, (side_a, side_b), keep_west, keep_east, -1.0)
        stores = []
        for i in range(ND):
            passed = jnp.maximum(fc * SIN[i] - their_v, 0.0) * their_sea
            back = fetch(sent_ref, group, base, mirrored(i))
            from_cross = fetch(cross_in, group, base, i) + passed * back
            from_rows = [
                sea_cross * from_cross,
                sea[1] * fetch(chip_in, group, base, mirrored(i)),
            ]
            for r in range(2):
                from_cols = sea_rim[r] * brought(border[r], i)
                new = part_ref[field_rows(group, r, i), :] + from_rows[r] + from_cols
                i_to = jnp.where(odd == 1, 2 * mirrored(i), 2 * i)
                r_to = jnp.where(odd == 1, 1 - r, r)
                stores.append((work, pl.ds(group * CHUNK + i_to + r_to, SUB, stride=2 * ND), new))
            if i % BATCH == BATCH - 1:
                flush(stores)
        chunk(group).start()

    each_group(finish)
    for group in range(LAST):
        chunk(group).wait()
    chunk(LAST).wait()


VMEM = pl.BlockSpec(memory_space=pltpu.VMEM)
HBM = pl.BlockSpec(memory_space=pltpu.HBM)
PARAMS = pltpu.CompilerParams(vmem_limit_bytes=24 * 1024 * 1024)


def shape(rows):
    return jax.ShapeDtypeStruct((rows, LANES), F32)


def call(kernel, outs, name, *args, span=0):
    return pl.pallas_call(
        kernel,
        out_shape=[shape(rows) for rows in outs],
        in_specs=[VMEM] * len(args),
        out_specs=[VMEM] * len(outs),
        compiler_params=PARAMS,
        cost_estimate=pl.CostEstimate(flops=span, transcendentals=0, bytes_accessed=0),
        name=name,
    )(*args)


def both(pairs):
    return pairs + [(b, a) for a, b in pairs]


def swap_cross(packet):
    geo, spec = lax.axis_size("geo"), lax.axis_size("spec")
    place = lambda row, col: row * spec + col
    links = [(place(k, c), place(k + 1, c)) for k in range(1, geo - 1, 2) for c in range(spec)]
    links += [(place(k, c), place(k, c + 1)) for k in (0, geo - 1) for c in range(0, spec, 2)]
    return lax.ppermute(packet, ("geo", "spec"), both(links))


def swap_chip(packet):
    cores = [(k, k + 1) for k in range(0, lax.axis_size("geo"), 2)]
    return lax.ppermute(packet, "geo", both(cores))


def swap_columns(side):
    geo, spec = lax.axis_size("geo"), lax.axis_size("spec")
    place = lambda row, col: row * spec + col
    inner = [(place(k, c), place(k, c + 1)) for k in range(geo) for c in range(0, spec, 2)]
    outer = [(place(k, c), place(k, c + 1)) for k in range(geo) for c in range(1, spec - 1, 2)]
    outer += [(place(k, c), place(k + 1, c)) for k in range(0, geo, 2) for c in (0, spec - 1)]
    return [lax.ppermute(side, ("geo", "spec"), both(pairs)) for pairs in (inner, outer)]


def per_device(
    spectrum, wind_speed, wind_dir, current_u, current_v, refract_x, refract_y, land_mask
):
    rows = spectrum.shape[0] * spectrum.shape[1] * spectrum.shape[2]
    flat = spectrum.reshape(rows, LANES)
    inputs = [flat, wind_speed, wind_dir, current_u, current_v, refract_x, refract_y, land_mask]
    inputs = [pltpu.with_memory_space_constraint(value, pltpu.HBM) for value in inputs]
    energy, cross, side, fields = pl.pallas_call(
        source_kernel,
        out_shape=[shape(n) for n in (FIELD, PACKET, SIDE, FIELDS)],
        in_specs=[HBM] * len(inputs),
        out_specs=[VMEM] * 4,
        scratch_shapes=[pltpu.VMEM((PADF * 2 * ND, LANES), F32)]
        + [pltpu.VMEM(value.shape, value.dtype) for value in inputs[1:]]
        + [pltpu.SemaphoreType.DMA((GROUPS + len(inputs) - 1,))],
        compiler_params=PARAMS,
        name="source",
    )(*inputs)
    sides = swap_columns(side)
    cross_in = swap_cross(cross)
    part, late, chip = call(
        functools.partial(transport_kernel, True),
        (FIELD, PACKET + SUB, PACKET),
        "first_substep",
        energy,
        *sides,
        fields,
        span=SPAN,
    )
    late_in = swap_cross(late)
    chip_in = swap_chip(chip)
    energy, chip, side = call(
        complete_kernel, (FIELD, PACKET, SIDE), "complete", part, cross_in, chip_in, fields
    )
    sides = swap_columns(side)
    chip_in = swap_chip(chip)
    (part,) = call(
        functools.partial(transport_kernel, False), (FIELD,), "second_substep", energy, fields
    )
    out = pl.pallas_call(
        finish_kernel,
        out_shape=shape(rows),
        in_specs=[VMEM] * 7,
        out_specs=HBM,
        scratch_shapes=[
            pltpu.VMEM((PADF * 2 * ND, LANES), F32),
            pltpu.SemaphoreType.DMA((GROUPS,)),
        ],
        compiler_params=PARAMS,
        name="finish",
    )(part, cross, late_in, chip_in, *sides, fields)
    return out.reshape(spectrum.shape)


def solution(mesh):
    in_specs = (
        P(None, None, "geo", "spec"),
        P("geo", "spec"),
        P("geo", "spec"),
        P("geo", None),
        P("geo", None),
        P("geo", None),
        P("geo", None),
        P("geo", None),
    )
    out_specs = P(None, None, "geo", "spec")
    return jax.shard_map(
        per_device, mesh=mesh, in_specs=in_specs, out_specs=out_specs, check_vma=False
    )
```

```python
import functools
import math

import jax
import jax.numpy as jnp
from jax import lax
from jax.experimental import pallas as pl
from jax.experimental.pallas import tpu as pltpu
from jax.sharding import PartitionSpec as P

gravity = 9.81
lowest_radian = 2.0 * math.pi * 0.0373
log_span = 49.0 * math.log(1.1)
wind_coef = 1.7e-06
break_coef = 2.5e-05
steep_ref = 480.0
wind_factor = 1.1
source_seconds = 360.0
courant_cells = 0.02
substep_seconds = 180.0

NF = 50
ND = 36
LANES = 128
SUB = 8
GROUPS = 7
PADF = SUB * GROUPS
RATIO = log_span / (NF - 1)
DTH = 2.0 * math.pi / ND
COS = [math.cos(DTH * i) for i in range(ND)]
SIN = [math.sin(DTH * i) for i in range(ND)]
GSPEED = [gravity / (2.0 * lowest_radian * math.exp(RATIO * j)) for j in range(NF)]
FIRST = [
    min(j for j in range(NF) if GSPEED[j] * SIN[i] > -1.001) // SUB for i in range(ND)
]
RANK = [0] * ND
for place, i_of in enumerate(sorted(range(ND), key=lambda i: (FIRST[i], i))):
    RANK[i_of] = place
COUNT = [sum(1 for i in range(ND) if FIRST[i] <= g) for g in range(GROUPS)]
BASE = [SUB * sum(COUNT[:g]) for g in range(GROUPS)]
TAIL = NF - SUB * (GROUPS - 1)
FIT = SUB // TAIL
SPARE = BASE[-1] + SUB * (ND // FIT)
PACKET = SPARE + SUB
TURN = 8
FIELDS = TURN + 2 * ND
BATCH = 3
FAR_BATCH = 6
SPAN = 2 * 10**10
CHUNK = SUB * 2 * ND
FIELD = 2 * ND * PADF
SIDE = 2 * PADF
F32 = jnp.float32


def mirrored(i):
    return (ND - i) % ND


LAST = GROUPS - 1


def group_base(group):
    if group is LAST:
        return BASE[-1]
    total = 0
    for g in range(GROUPS - 1):
        total = total + jnp.where(group > g, SUB * COUNT[g], 0)
    return total


def slot(base, group, i):
    place = base + SUB * RANK[i]
    if FIRST[i] > 0:
        place = jnp.where(group >= FIRST[i], place, SPARE)
    return aligned(place)


def aligned(start):
    return pl.ds(start if isinstance(start, int) else pl.multiple_of(start, SUB), SUB)


def field_rows(group, r, i):
    return aligned((r * ND + i) * PADF + group * SUB)


def side_rows(group, r):
    return aligned(r * PADF + group * SUB)


def fetch(ref, group, base, i):
    if group is LAST:
        got = ref[aligned(BASE[-1] + SUB * (RANK[i] // FIT)), :]
        return pltpu.roll(got, (SUB - TAIL * (RANK[i] % FIT)) % SUB, 0)
    return ref[slot(base, group, i), :]


class Sender:
    def __init__(self, ref, group, base):
        self.ref, self.group, self.base, self.shared = ref, group, base, {}

    def put(self, i, value):
        if self.group is not LAST:
            return [(self.ref, slot(self.base, self.group, i), value)]
        block, part = RANK[i] // FIT, RANK[i] % FIT
        held = self.shared.setdefault(block, {})
        held[part] = pltpu.roll(value, TAIL * part, 0) if part else value
        if len(held) < FIT:
            return []
        place = lax.broadcasted_iota(jnp.int32, (SUB, LANES), 0)
        full = held[FIT - 1]
        for part in range(FIT - 1):
            inside = (place >= TAIL * part) & (place < TAIL * (part + 1))
            full = jnp.where(inside, held[part], full)
        return [(self.ref, aligned(BASE[-1] + SUB * block), full)]


def radian_of(group):
    j = lax.broadcasted_iota(jnp.int32, (SUB, LANES), 0) + group * SUB
    return lowest_radian * jnp.exp(j.astype(F32) * RATIO), j


def position():
    odd = lax.rem(lax.axis_index("geo"), 2)
    col = pl.multiple_of(lax.axis_index("spec") * LANES, LANES)
    sign = jnp.where(odd == 1, -1.0, 1.0).astype(F32)
    return odd, col, sign


def inside():
    geo, spec = lax.axis_index("geo"), lax.axis_index("spec")
    first, last = lax.axis_size("geo") - 1, lax.axis_size("spec") - 1
    keep = lambda edge: jnp.where(edge, 0.0, 1.0).astype(F32)
    return keep((geo == 0) | (geo == first)), keep(spec == 0), keep(spec == last)


def row_of(ref, odd, r, col):
    window = (ref[...] if col is None else ref[:, pl.ds(col, LANES)]).astype(F32)
    first, second = window[0:1], window[1:2]
    own, other = (first, second) if r == 0 else (second, first)
    return jnp.where(odd == 1, other, own)


def spread(row):
    return jnp.broadcast_to(row, (SUB, LANES))


def lane_ids():
    return lax.broadcasted_iota(jnp.int32, (SUB, LANES), 1)


class Gather:
    def __init__(self, lane):
        self.lane, self.pair = lane, lax.shift_right_logical(lane + 1, 1)
        self.total = [jnp.zeros((SUB, LANES), F32)] * 2
        self.queue = []

    def put(self, i, energy, cx):
        flux = []
        for r in range(2):
            speed = jnp.where(self.lane == 0, jnp.minimum(cx[r], 0.0), jnp.maximum(cx[r], 0.0))
            flux.append(speed * energy[r])
        self.queue.append((i, flux))

    def finish(self, side_ref, group):
        for i, flux in self.queue:
            for r in range(2):
                moved = pltpu.roll(flux[r], 2 * i + 2, 1)
                self.total[r] = jnp.where(self.pair == i + 1, moved, self.total[r])
        for r in range(2):
            side_ref[side_rows(group, r), :] = self.total[r]


def cross_flux(cy, energy):
    return jnp.maximum(-cy, 0.0) * energy


def chip_flux(cy, energy):
    return jnp.maximum(cy, 0.0) * energy


def flush(stores):
    for ref, rows, value in stores:
        ref[rows, :] = value
    stores.clear()


def each_group(body):
    lax.fori_loop(0, LAST, lambda group, carry: body(group) or carry, 0)
    body(LAST)


def finish_packet(ref):
    ref[SPARE:PACKET, :] = jnp.zeros((SUB, LANES), F32)


def field_of(fields_ref, kind):
    return [spread(fields_ref[2 * kind + r : 2 * kind + r + 1, :]) for r in range(2)]


def source_kernel(*refs):
    inputs, refs = refs[:8], refs[8:]
    e_ref, cross_ref, side_ref, fields_ref, raw = refs[:5]
    held, sems = refs[5:12], refs[12]
    odd, col, sign = position()
    copies = [
        pltpu.make_async_copy(source, target, sems.at[GROUPS + k])
        for k, (source, target) in enumerate(zip(inputs[1:], held))
    ]

    def chunk(group, size):
        rows = pl.ds(group * CHUNK, size)
        return pltpu.make_async_copy(inputs[0].at[rows], raw.at[rows], sems.at[group])

    final = chunk(LAST, TAIL * 2 * ND)
    for group in range(LAST):
        chunk(group, CHUNK).start()
    final.start()
    for copy in copies:
        copy.start()
    raw[NF * 2 * ND :, :] = jnp.zeros(((PADF - NF) * 2 * ND, LANES), F32)
    ws_ref, wd_ref, u_ref, v_ref, rx_ref, ry_ref, sea_ref = held

    def stats(group, sums):
        if group is LAST:
            final.wait()
        else:
            chunk(group, CHUNK).wait()
        s, j = radian_of(group)
        valid = j < NF
        w1 = jnp.where(valid, s * ((math.exp(RATIO) - 1.0) * DTH), 0.0)
        w2 = jnp.where(valid, (math.exp(RATIO) - 1.0) * DTH, 0.0)
        out = []
        for r in range(2):
            parts = [None, None, None, None]
            r_from = jnp.where(odd == 1, 1 - r, r)
            stores = []
            for i in range(ND):
                i_from = jnp.where(odd == 1, 2 * mirrored(i), 2 * i)
                got = raw[pl.ds(group * CHUNK + i_from + r_from, SUB, stride=2 * ND), :]
                stores.append((e_ref, field_rows(group, r, i), got))
                k = i % 4
                parts[k] = got if parts[k] is None else parts[k] + got
                if i % 9 == 8:
                    flush(stores)
            part = (parts[0] + parts[1]) + (parts[2] + parts[3])
            out.append((sums[r][0] + part * w1, sums[r][1] + part * w2))
        return tuple(out)

    blank = jnp.zeros((SUB, LANES), F32)
    sums = stats(LAST, lax.fori_loop(0, LAST, stats, ((blank, blank), (blank, blank))))
    for copy in copies:
        copy.wait()
    wind_x, wind_y, sea, decay, u = [], [], [], [], []
    for r in range(2):
        total = jnp.sum(sums[r][0], axis=0, keepdims=True)
        inverse = jnp.sum(sums[r][1], axis=0, keepdims=True)
        mean_sigma = total / inverse
        mean_k = mean_sigma * mean_sigma / gravity
        ratio = total * mean_k * mean_k / steep_ref
        decay.append(spread(source_seconds * break_coef * ratio * ratio / mean_sigma))
        strength = row_of(ws_ref, odd, r, None) * (wind_factor / gravity)
        angle = row_of(wd_ref, odd, r, None) * sign
        wind_x.append(spread(strength * jnp.cos(angle)))
        wind_y.append(spread(strength * jnp.sin(angle)))
        own = [
            row_of(sea_ref, odd, r, col),
            courant_cells * row_of(u_ref, odd, r, col),
            courant_cells * sign * row_of(v_ref, odd, r, col),
        ]
        for k in range(3):
            fields_ref[2 * k + r : 2 * k + r + 1, :] = own[k]
        sea.append(spread(own[0]))
        u.append(spread(own[1]))
        if r == 0:
            v = spread(own[2])
        rx = row_of(rx_ref, odd, r, col)
        ry = sign * row_of(ry_ref, odd, r, col)
        for i in range(ND):
            at = TURN + r * ND + i
            fields_ref[at : at + 1, :] = SIN[i] * rx - COS[i] * ry
    lane = lane_ids()

    def source(group):
        s, _ = radian_of(group)
        fc = (courant_cells * gravity / 2.0) / s
        gain = s * (source_seconds * wind_coef)
        damp = [sea[r] / (1.0 + decay[r] * s * s) for r in range(2)]
        base = group_base(group)
        cross = Sender(cross_ref, group, base)
        gather, stores = Gather(lane), []
        for i in range(ND):
            energy, cx = [], []
            for r in range(2):
                rows = field_rows(group, r, i)
                align = wind_x[r] * COS[i] + wind_y[r] * SIN[i]
                growth = gain * jnp.maximum(s * align - 1.0, 0.0)
                new = e_ref[rows, :] * damp[r] * (1.0 + growth)
                stores.append((e_ref, rows, new))
                energy.append(new)
                cx.append(fc * COS[i] + u[r])
            gather.put(i, energy, cx)
            stores += cross.put(mirrored(i), cross_flux(fc * SIN[i] + v, energy[0]))
            if i % BATCH == BATCH - 1:
                flush(stores)
        gather.finish(side_ref, group)

    each_group(source)
    finish_packet(cross_ref)


def borders(group, sides, keep_west, keep_east, sign):
    odd_lane = lax.rem(lane_ids(), 2) == 1
    even_col = lax.rem(lax.axis_index("spec"), 2) == 0
    out = []
    for r in range(2):
        second, first = [ref[side_rows(group, r), :] for ref in sides]
        from_west = keep_west * jnp.where(even_col, second, first)
        from_east = (sign * keep_east) * jnp.where(even_col, first, second)
        from_east = pltpu.roll(from_east, LANES - 2, 1)
        out.append(jnp.where(odd_lane, from_west, from_east))
    return out


def brought(border, i):
    return pltpu.roll(border, (LANES - (2 * i + 1)) % LANES, 1)


def speeds(group):
    s, _ = radian_of(group)
    c = (gravity / 2.0) / s
    return courant_cells * c, (substep_seconds / DTH) * c


def transport_kernel(first_step, *refs):
    if first_step:
        e_ref, *sides, fields_ref, out_ref, cross_ref, chip_ref = refs
    else:
        e_ref, fields_ref, out_ref = refs
    _, keep_west, keep_east = inside()
    sea, u, v = [field_of(fields_ref, kind) for kind in range(3)]
    lane = lane_ids()

    def substep(group):
        fc, tc = speeds(group)
        if first_step:
            base = group_base(group)
            border = borders(group, sides, keep_west, keep_east, 1.0)
            cross, chip = Sender(cross_ref, group, base), Sender(chip_ref, group, base)

        def turned(r, i):
            energy = e_ref[field_rows(group, r, i), :]
            at = TURN + r * ND + i
            speed = tc * spread(fields_ref[at : at + 1, :])
            return energy, jnp.maximum(speed, 0.0) * energy, jnp.minimum(speed, 0.0) * energy

        before = [turned(r, ND - 1)[1] for r in range(2)]
        first = [turned(r, 0) for r in range(2)]
        here = first
        stores = []
        for i in range(ND):
            after = [turned(r, i + 1) for r in range(2)] if i + 1 < ND else first
            cx = [fc * COS[i] + u[r] for r in range(2)]
            cy = [fc * SIN[i] + v[r] for r in range(2)]
            energy = [here[r][0] for r in range(2)]
            py = [jnp.maximum(cy[r], 0.0) * energy[r] for r in range(2)]
            my = [jnp.minimum(cy[r], 0.0) * energy[r] for r in range(2)]
            in_y = [-my[1], py[0]]
            new = []
            for r in range(2):
                px = jnp.maximum(cx[r], 0.0) * energy[r]
                mx = jnp.minimum(cx[r], 0.0) * energy[r]
                edge = brought(border[r], i) if first_step else 0.0
                px_in = jnp.where(lane == 0, edge, pltpu.roll(px, 1, 1))
                mx_in = jnp.where(lane == LANES - 1, edge, pltpu.roll(mx, LANES - 1, 1))
                stay = energy[r] - (px - mx) - (py[r] - my[r]) - (here[r][1] - here[r][2])
                gained = (px_in - mx_in) + in_y[r] + (before[r] - after[r][2])
                new.append(sea[r] * (stay + gained))
            for r in range(2):
                stores.append((out_ref, field_rows(group, r, i), new[r]))
            if first_step:
                stores += cross.put(mirrored(i), cross_flux(cy[0], new[0]))
                stores += chip.put(i, py[1])
            if i % BATCH == BATCH - 1:
                flush(stores)
            before = [here[r][1] for r in range(2)]
            here = after

    each_group(substep)
    if first_step:
        finish_packet(cross_ref)
        finish_packet(chip_ref)
        cross_ref[PACKET:, :] = jnp.zeros((SUB, LANES), F32)
        cross_ref[PACKET : PACKET + 1, :] = fields_ref[0:1, :]
        cross_ref[PACKET + 1 : PACKET + 2, :] = fields_ref[4:5, :]


def complete_kernel(part_ref, cross_in, chip_in, fields_ref, e_ref, chip_ref, side_ref):
    keep_cross, _, _ = inside()
    sea, u, v = [field_of(fields_ref, kind) for kind in range(3)]
    sea_cross = keep_cross * sea[0]
    lane = lane_ids()

    def complete(group):
        fc, _ = speeds(group)
        base = group_base(group)
        chip, gather, stores = Sender(chip_ref, group, base), Gather(lane), []
        for i in range(ND):
            rows = [field_rows(group, r, i) for r in range(2)]
            new = [
                part_ref[rows[0], :] + sea_cross * fetch(cross_in, group, base, i),
                part_ref[rows[1], :] + sea[1] * fetch(chip_in, group, base, mirrored(i)),
            ]
            gather.put(i, new, [fc * COS[i] + u[r] for r in range(2)])
            for r in range(2):
                stores.append((e_ref, rows[r], new[r]))
            stores += chip.put(i, chip_flux(fc * SIN[i] + v[1], new[1]))
            if i % BATCH == BATCH - 1:
                flush(stores)
        gather.finish(side_ref, group)

    each_group(complete)
    finish_packet(chip_ref)


def places(group, r, i, odd):
    i_to = jnp.where(odd == 1, 2 * mirrored(i), 2 * i)
    r_to = jnp.where(odd == 1, 1 - r, r)
    return pl.ds(group * CHUNK + i_to + r_to, SUB, stride=2 * ND)


def near_kernel(part_ref, chip_in, side_a, side_b, fields_ref, out_ref):
    _, keep_west, keep_east = inside()
    sea = field_of(fields_ref, 0)
    lane = lane_ids()
    rim = jnp.where((lane == 0) | (lane == LANES - 1), 1.0, 0.0)
    sea_rim = [sea[r] * rim for r in range(2)]

    def near(group):
        base = group_base(group)
        border = borders(group, (side_a, side_b), keep_west, keep_east, -1.0)
        stores = []
        for i in range(ND):
            for r in range(2):
                rows = field_rows(group, r, i)
                new = part_ref[rows, :] + sea_rim[r] * brought(border[r], i)
                if r == 1:
                    new = new + sea[1] * fetch(chip_in, group, base, mirrored(i))
                stores.append((out_ref, rows, new))
            if i % BATCH == BATCH - 1:
                flush(stores)

    each_group(near)


def far_kernel(part_ref, sent_ref, cross_in, fields_ref, out_hbm, work, sems):
    odd, _, _ = position()
    keep_cross, _, _ = inside()
    sea_cross = keep_cross * field_of(fields_ref, 0)[0]
    their_sea = spread(cross_in[PACKET : PACKET + 1, :])
    their_v = spread(cross_in[PACKET + 1 : PACKET + 2, :])

    def chunk(group):
        rows = pl.ds(group * CHUNK, TAIL * 2 * ND if group is LAST else CHUNK)
        return pltpu.make_async_copy(work.at[rows], out_hbm.at[rows], sems.at[group])

    def far(group):
        fc, _ = speeds(group)
        base = group_base(group)
        stores = []
        for i in range(ND):
            passed = jnp.maximum(fc * SIN[i] - their_v, 0.0) * their_sea
            back = fetch(sent_ref, group, base, mirrored(i))
            from_cross = fetch(cross_in, group, base, i) + passed * back
            new = [part_ref[field_rows(group, r, i), :] for r in range(2)]
            new[0] = new[0] + sea_cross * from_cross
            for r in range(2):
                stores.append((work, places(group, r, i, odd), new[r]))
            if i % FAR_BATCH == FAR_BATCH - 1:
                flush(stores)
        chunk(group).start()

    each_group(far)
    for group in range(LAST):
        chunk(group).wait()
    chunk(LAST).wait()


VMEM = pl.BlockSpec(memory_space=pltpu.VMEM)
HBM = pl.BlockSpec(memory_space=pltpu.HBM)
PARAMS = pltpu.CompilerParams(vmem_limit_bytes=24 * 1024 * 1024)


def shape(rows):
    return jax.ShapeDtypeStruct((rows, LANES), F32)


def call(kernel, outs, name, *args, span=0):
    return pl.pallas_call(
        kernel,
        out_shape=[shape(rows) for rows in outs],
        in_specs=[VMEM] * len(args),
        out_specs=[VMEM] * len(outs),
        compiler_params=PARAMS,
        cost_estimate=pl.CostEstimate(flops=span, transcendentals=0, bytes_accessed=0),
        name=name,
    )(*args)


def both(pairs):
    return pairs + [(b, a) for a, b in pairs]


def swap_cross(packet):
    geo, spec = lax.axis_size("geo"), lax.axis_size("spec")
    place = lambda row, col: row * spec + col
    links = [(place(k, c), place(k + 1, c)) for k in range(1, geo - 1, 2) for c in range(spec)]
    links += [(place(k, c), place(k, c + 1)) for k in (0, geo - 1) for c in range(0, spec, 2)]
    return lax.ppermute(packet, ("geo", "spec"), both(links))


def swap_chip(packet):
    cores = [(k, k + 1) for k in range(0, lax.axis_size("geo"), 2)]
    return lax.ppermute(packet, "geo", both(cores))


def swap_columns(side):
    geo, spec = lax.axis_size("geo"), lax.axis_size("spec")
    place = lambda row, col: row * spec + col
    inner = [(place(k, c), place(k, c + 1)) for k in range(geo) for c in range(0, spec, 2)]
    outer = [(place(k, c), place(k, c + 1)) for k in range(geo) for c in range(1, spec - 1, 2)]
    outer += [(place(k, c), place(k + 1, c)) for k in range(0, geo, 2) for c in (0, spec - 1)]
    return [lax.ppermute(side, ("geo", "spec"), both(pairs)) for pairs in (outer, inner)]


def per_device(
    spectrum, wind_speed, wind_dir, current_u, current_v, refract_x, refract_y, land_mask
):
    rows = spectrum.shape[0] * spectrum.shape[1] * spectrum.shape[2]
    flat = spectrum.reshape(rows, LANES)
    inputs = [flat, wind_speed, wind_dir, current_u, current_v, refract_x, refract_y, land_mask]
    inputs = [pltpu.with_memory_space_constraint(value, pltpu.HBM) for value in inputs]
    energy, cross, side, fields = pl.pallas_call(
        source_kernel,
        out_shape=[shape(n) for n in (FIELD, PACKET, SIDE, FIELDS)],
        in_specs=[HBM] * len(inputs),
        out_specs=[VMEM] * 4,
        scratch_shapes=[pltpu.VMEM((PADF * 2 * ND, LANES), F32)]
        + [pltpu.VMEM(value.shape, value.dtype) for value in inputs[1:]]
        + [pltpu.SemaphoreType.DMA((GROUPS + len(inputs) - 1,))],
        compiler_params=PARAMS,
        name="source",
    )(*inputs)
    sides = swap_columns(side)
    cross_in = swap_cross(cross)
    part, late, chip = call(
        functools.partial(transport_kernel, True),
        (FIELD, PACKET + SUB, PACKET),
        "first_substep",
        energy,
        *sides,
        fields,
        span=SPAN,
    )
    late_in = swap_cross(late)
    chip_in = swap_chip(chip)
    energy, chip, side = call(
        complete_kernel, (FIELD, PACKET, SIDE), "complete", part, cross_in, chip_in, fields
    )
    sides = swap_columns(side)
    chip_in = swap_chip(chip)
    (part,) = call(
        functools.partial(transport_kernel, False), (FIELD,), "second_substep", energy, fields
    )
    (part,) = call(near_kernel, (FIELD,), "near_flux", part, chip_in, *sides, fields)
    out = pl.pallas_call(
        far_kernel,
        out_shape=shape(rows),
        in_specs=[VMEM] * 4,
        out_specs=HBM,
        scratch_shapes=[
            pltpu.VMEM((PADF * 2 * ND, LANES), F32),
            pltpu.SemaphoreType.DMA((GROUPS,)),
        ],
        compiler_params=PARAMS,
        name="far_flux",
    )(part, cross, late_in, fields)
    return out.reshape(spectrum.shape)


def solution(mesh):
    in_specs = (
        P(None, None, "geo", "spec"),
        P("geo", "spec"),
        P("geo", "spec"),
        P("geo", None),
        P("geo", None),
        P("geo", None),
        P("geo", None),
        P("geo", None),
    )
    out_specs = P(None, None, "geo", "spec")
    return jax.shard_map(
        per_device, mesh=mesh, in_specs=in_specs, out_specs=out_specs, check_vma=False
    )
```
